32 devices in a mesh: outer: 2 (over y), inner: 4 (over z), tensor: 4 (over x, core).
Axes of the slice: x: 2, y: 2, z: 4, core: 2. Of those that a mesh axis runs over, the one named last changes fastest.
Arguments:
- queries: bfloat16 [1024, 4096], P(('outer', 'inner'), 'tensor'), may hold values from -12 to 12
- keys: bfloat16 [1024, 512], P(('outer', 'inner'), 'tensor'), may hold values from -12 to 12
- values: bfloat16 [1024, 512], P(('outer', 'inner'), 'tensor'), may hold values from -6 to 6
- ancestors: int32 [8, 4], P(('outer', 'inner')), may hold values from -1 to 7, as said below
- visible_cut: int32 [8, 4], P(('outer', 'inner')), may hold values from 0 to 128, as said below
- positions: int32 [1024], P(('outer', 'inner')), may hold values from 0 to 511, as said below
Outputs:
- attention: bfloat16 [1024, 4096], P(('outer', 'inner', 'tensor'))
The draws below stay inside these ranges and needn't reach their ends.
Inputs may be any that keep to these rules, and one draw needn't show every extreme that they name: `ancestors`: row i lists block i first, then its parent, the parent's parent and so on to block 0, padded with -1; every parent has a smaller index than its child; some row is full in every draw. `visible_cut`: entry 0 of each row is 128; entry e >= 1 is the offset at which the path leaves block ancestors[i, e], that is the offset of the child of that block on the path; padding entries are 0. Block i's first token sits at its parent's first position plus visible_cut[i, 1] (block 0 starts at 0); positions rise by one inside a block.
All inputs are finite; a program needn't handle non-finite values.
Results may differ from the reference program's by a relative error of at most 0.012.
The reference program's roundings to bfloat16 on the way count: a program that leaves them out, or rounds other values in their place, can miss the bound.
Values may be sent and summed in bfloat16 or wider, within the bound.
A program may use at most 64 MiB of HBM per device.

```python
import math
import jax
import jax.numpy as jnp
from jax import lax

QUERY_HEAD_COUNT = 32
KEY_VALUE_HEADS = 4
HEAD_SIZE = 128
TREE_BLOCK_SIZE = 128
PACKED_TOKENS = 1024
ANC_MAX = 4


def tree_parts(key):
    tree_block_count = PACKED_TOKENS // TREE_BLOCK_SIZE
    spine_coin = jax.random.randint(jax.random.fold_in(key, 11), (tree_block_count,), 0, 2)
    jump_draw = jax.random.randint(jax.random.fold_in(key, 12), (tree_block_count,), 0, 1 << 30)
    offset_draw = jax.random.randint(jax.random.fold_in(key, 13), (tree_block_count,), 1, TREE_BLOCK_SIZE + 1)
    near_coin = jax.random.randint(jax.random.fold_in(key, 14), (tree_block_count,), 0, 2)

    def grow(state, blk_id):
        parents, depths, starts, block_lists, cut_lists, last_spine, spine_count = state
        gap = blk_id - last_spine
        on_spine = (blk_id > 0) & (spine_count < ANC_MAX) & ((gap >= 2) | (spine_coin[blk_id] == 1))
        jump_to = jump_draw[blk_id] % jnp.maximum(blk_id, 1)
        loose = jnp.where(near_coin[blk_id] == 1, blk_id - 1, jump_to)
        loose = jnp.maximum(loose, 0)
        loose = jnp.where(depths[loose] >= ANC_MAX, jnp.maximum(parents[loose], 0), loose)
        chosen = jnp.where(on_spine, last_spine, loose)
        offset = jnp.where(on_spine, TREE_BLOCK_SIZE, offset_draw[blk_id])
        offset = jnp.where(blk_id == 0, 0, offset)
        own_depth = jnp.where(blk_id == 0, 1, depths[chosen] + 1)
        own_start = jnp.where(blk_id == 0, 0, starts[chosen] + offset)
        up_list = block_lists[chosen]
        up_cut = cut_lists[chosen]
        new_row = jnp.where(blk_id == 0, jnp.concatenate([jnp.zeros((1,), jnp.int32), jnp.full((ANC_MAX - 1,), -1, jnp.int32)]), jnp.concatenate([blk_id[None], up_list[:-1]]))
        new_cuts = jnp.where(blk_id == 0, jnp.concatenate([jnp.full((1,), TREE_BLOCK_SIZE, jnp.int32), jnp.zeros((ANC_MAX - 1,), jnp.int32)]), jnp.concatenate([jnp.full((1,), TREE_BLOCK_SIZE, jnp.int32), offset[None].astype(jnp.int32), up_cut[1:-1]]))
        parents = parents.at[blk_id].set(jnp.where(blk_id == 0, -1, chosen))
        depths = depths.at[blk_id].set(own_depth)
        starts = starts.at[blk_id].set(own_start)
        block_lists = block_lists.at[blk_id].set(new_row)
        cut_lists = cut_lists.at[blk_id].set(new_cuts)
        last_spine = jnp.where(on_spine, blk_id, last_spine)
        spine_count = jnp.where(on_spine, spine_count + 1, spine_count)
        return ((parents, depths, starts, block_lists, cut_lists, last_spine, spine_count), 0)
    initial = (jnp.full((tree_block_count,), -1, jnp.int32), jnp.zeros((tree_block_count,), jnp.int32), jnp.zeros((tree_block_count,), jnp.int32), jnp.full((tree_block_count, ANC_MAX), -1, jnp.int32), jnp.zeros((tree_block_count, ANC_MAX), jnp.int32), jnp.zeros((), jnp.int32), jnp.ones((), jnp.int32))
    final_state, unused = lax.scan(grow, initial, jnp.arange(tree_block_count, dtype=jnp.int32))
    return (final_state[2], final_state[3], final_state[4])


def draw_queries(key, part):
    self_key = jax.random.fold_in(key, 3)
    sampled_values = jnp.clip(1.5 * jax.random.normal(self_key, (PACKED_TOKENS, QUERY_HEAD_COUNT * HEAD_SIZE), jnp.float32), -12.0, 12.0)
    return sampled_values.astype(jnp.bfloat16)


def draw_keys(key, part):
    self_key = jax.random.fold_in(key, 4)
    sampled_values = jnp.clip(1.5 * jax.random.normal(self_key, (PACKED_TOKENS, KEY_VALUE_HEADS * HEAD_SIZE), jnp.float32), -12.0, 12.0)
    return sampled_values.astype(jnp.bfloat16)


def draw_ancestors(key, part):
    starts, block_lists, cut_lists = tree_parts(key)
    return block_lists


def draw_visible_cut(key, part):
    starts, block_lists, cut_lists = tree_parts(key)
    return cut_lists


def draw_positions(key, part):
    starts, block_lists, cut_lists = tree_parts(key)
    token_ids = jnp.arange(PACKED_TOKENS, dtype=jnp.int32)
    return (starts[token_ids // TREE_BLOCK_SIZE] + token_ids % TREE_BLOCK_SIZE).astype(jnp.int32)


def levels(key, extent, split, least, top_value):
    def one(position, blocks):
        heights = jax.random.uniform(jax.random.fold_in(jax.random.fold_in(key, 6), position), (blocks,), jnp.float32, least / len(split), top_value / len(split))
        return jnp.repeat(jnp.exp(heights), extent[position] // blocks).reshape((-1,) + (1,) * (len(extent) - position - 1))

    factor_of = one(*split[0])
    for cut in split[1:]:
        factor_of = factor_of * one(*cut)
    return factor_of


def scatter_about(own_key, extent, spread, reach, shards=(), held_as=jnp.bfloat16):
    array = jax.random.normal(own_key, extent, jnp.float32) * spread
    if len(shards) > 0:
        array = levels(own_key, extent, shards, -0.22, 0.18) * array
    return jnp.clip(array, min=-reach, max=reach).astype(held_as)


def setup_inputs(seed: int = 0) -> dict:
    streams_of = jax.random.split(jax.random.key(seed), 7)
    return {
        "queries": draw_queries(jax.random.fold_in(streams_of[6], 71), 0),
        "keys": draw_keys(jax.random.fold_in(streams_of[6], 71), 0),
        "values": scatter_about(streams_of[2], (PACKED_TOKENS, KEY_VALUE_HEADS * HEAD_SIZE), 1.0, 6.0, ((0, 8), (1, 4))),
        "ancestors": draw_ancestors(jax.random.fold_in(streams_of[6], 71), 0),
        "visible_cut": draw_visible_cut(jax.random.fold_in(streams_of[6], 71), 0),
        "positions": draw_positions(jax.random.fold_in(streams_of[6], 71), 0),
    }


rope_base = 500000.0

def apply_rotary(source, positions, head_count):
    token_count = source.shape[0]
    half_dim = HEAD_SIZE // 2
    frequency = jnp.exp(jnp.arange(half_dim, dtype=jnp.float32) * (-2.0 / HEAD_SIZE) * math.log(rope_base))
    angles = positions.astype(jnp.float32)[:, None] * frequency[None, :]
    cosines = jnp.cos(angles)[:, None, :]
    sine_vals = jnp.sin(angles)[:, None, :]
    split_heads = source.astype(jnp.float32).reshape(token_count, head_count, HEAD_SIZE)
    front_half = split_heads[..., :half_dim]
    back_half = split_heads[..., half_dim:]
    turned = jnp.concatenate([front_half * cosines - back_half * sine_vals, back_half * cosines + front_half * sine_vals], axis=-1)
    return turned.reshape(token_count, head_count * HEAD_SIZE).astype(jnp.bfloat16)

def reference(queries, keys, values, ancestors, visible_cut, positions):
    rotary_queries = apply_rotary(queries, positions, QUERY_HEAD_COUNT)
    rotary_keys = apply_rotary(keys, positions, KEY_VALUE_HEADS)
    tree_block_count = PACKED_TOKENS // TREE_BLOCK_SIZE
    head_group_width = QUERY_HEAD_COUNT // KEY_VALUE_HEADS
    scale = 1.0 / math.sqrt(HEAD_SIZE)
    key_block_rows = rotary_keys.reshape(tree_block_count, TREE_BLOCK_SIZE, KEY_VALUE_HEADS, HEAD_SIZE)
    value_block_rows = values.reshape(tree_block_count, TREE_BLOCK_SIZE, KEY_VALUE_HEADS, HEAD_SIZE)
    query_block_rows = rotary_queries.reshape(tree_block_count, TREE_BLOCK_SIZE, KEY_VALUE_HEADS, head_group_width, HEAD_SIZE)
    inside = jnp.arange(TREE_BLOCK_SIZE, dtype=jnp.int32)

    def one_block(packed):
        query_block, block_list, cut_list, query_id = packed
        safe_ids = jnp.maximum(block_list, 0)
        key_set = key_block_rows[safe_ids]
        val_set = value_block_rows[safe_ids]
        scores = jnp.einsum('skgd,aukd->kgsau', query_block.astype(jnp.float32), key_set.astype(jnp.float32)) * scale
        is_own = block_list == query_id
        within = inside[None, :] < cut_list[:, None]
        causal = inside[None, :] <= inside[:, None]
        visible = within[None, :, :] & (jnp.logical_not(is_own)[None, :, None] | causal[:, None, :])
        scores = jnp.where(visible[None, None], scores, -jnp.inf)
        row_max = lax.optimization_barrier(jnp.max(scores, axis=(3, 4)))
        exp_terms = jnp.exp(scores - row_max[..., None, None])
        total = lax.optimization_barrier(jnp.sum(exp_terms, axis=(3, 4)))
        weights = exp_terms.astype(jnp.bfloat16)
        summed = jnp.einsum('kgsau,aukd->skgd', weights.astype(jnp.float32), val_set.astype(jnp.float32))
        result = summed / jnp.transpose(total, (2, 0, 1))[..., None]
        return result.reshape(TREE_BLOCK_SIZE, QUERY_HEAD_COUNT * HEAD_SIZE).astype(jnp.bfloat16)
    outputs = lax.map(one_block, (query_block_rows, ancestors, visible_cut, jnp.arange(tree_block_count, dtype=jnp.int32)))
    return outputs.reshape(PACKED_TOKENS, QUERY_HEAD_COUNT * HEAD_SIZE)
```

```python
import functools
import math

import jax
import jax.numpy as jnp
from jax import lax
from jax.experimental import pallas as pl
from jax.experimental.pallas import tpu as pltpu
from jax.sharding import PartitionSpec as P

HEAD_SIZE = 128
TREE_BLOCK_SIZE = 128


rope_base = 500000.0
masked_low = -1e30


def apply_rotary(source, positions, head_count):
    token_count = source.shape[0]
    half_dim = HEAD_SIZE // 2
    frequency = jnp.exp(
        jnp.arange(half_dim, dtype=jnp.float32) * (-2.0 / HEAD_SIZE) * math.log(rope_base)
    )
    angles = positions.astype(jnp.float32)[:, None] * frequency[None, :]
    cosines = jnp.cos(angles)[:, None, :]
    sine_vals = jnp.sin(angles)[:, None, :]
    split_heads = source.astype(jnp.float32).reshape(token_count, head_count, HEAD_SIZE)
    front_half = split_heads[..., :half_dim]
    back_half = split_heads[..., half_dim:]
    turned = jnp.concatenate(
        [
            front_half * cosines - back_half * sine_vals,
            back_half * cosines + front_half * sine_vals,
        ],
        axis=-1,
    )
    return turned.reshape(token_count, head_count * HEAD_SIZE).astype(jnp.bfloat16)


def local(queries, keys, values, ancestors, visible_cut, positions):
    row_count = queries.shape[0]
    query_heads = queries.shape[1] // HEAD_SIZE
    kv_heads = keys.shape[1] // HEAD_SIZE
    head_group_width = query_heads // kv_heads
    scale = 1.0 / math.sqrt(HEAD_SIZE)
    rotary_queries = apply_rotary(queries, positions, query_heads)
    rotary_keys = apply_rotary(keys, positions, kv_heads)
    query_grid = rotary_queries.reshape(row_count, kv_heads, head_group_width, HEAD_SIZE)
    first_block = lax.axis_index(("outer", "inner")) * (row_count // TREE_BLOCK_SIZE)
    query_block = first_block + jnp.arange(row_count, dtype=jnp.int32) // TREE_BLOCK_SIZE
    query_inside = jnp.arange(row_count, dtype=jnp.int32) % TREE_BLOCK_SIZE
    key_inside = jnp.arange(TREE_BLOCK_SIZE, dtype=jnp.int32)

    def key_block_step(carried, key_block, val_block, key_id):
        cut_len = jnp.sum(jnp.where(ancestors == key_id, visible_cut, 0), axis=1)
        cut_rows = jnp.repeat(cut_len, TREE_BLOCK_SIZE)
        own_block = query_block == key_id
        visible = (key_inside[None, :] < cut_rows[:, None]) & (
            jnp.logical_not(own_block)[:, None] | (key_inside[None, :] <= query_inside[:, None])
        )

        def compute(state):
            running, total, weighted = state
            scores = (
                jnp.einsum(
                    "tkgd,skd->kgts",
                    query_grid,
                    key_block.reshape(TREE_BLOCK_SIZE, kv_heads, HEAD_SIZE),
                    preferred_element_type=jnp.float32,
                )
                * scale
            )
            scores = jnp.where(visible[None, None], scores, masked_low)
            new_max = jnp.maximum(running, jnp.max(scores, axis=-1))
            exp_terms = jnp.where(visible[None, None], jnp.exp(scores - new_max[..., None]), 0.0)
            rescale = jnp.exp(running - new_max)
            total = total * rescale + jnp.sum(exp_terms, axis=-1)
            weights = exp_terms.astype(jnp.bfloat16)
            update = jnp.einsum(
                "kgts,skd->tkgd",
                weights,
                val_block.reshape(TREE_BLOCK_SIZE, kv_heads, HEAD_SIZE),
                preferred_element_type=jnp.float32,
            )
            weighted = weighted * jnp.transpose(rescale, (2, 0, 1))[..., None] + update
            return (new_max, total, weighted)

        return lax.cond(jnp.any(visible), compute, lambda unchanged: unchanged, carried)

    initial = (
        jnp.full((kv_heads, head_group_width, row_count), masked_low, jnp.float32),
        jnp.zeros((kv_heads, head_group_width, row_count), jnp.float32),
        jnp.zeros((row_count, kv_heads, head_group_width, HEAD_SIZE), jnp.float32),
    )
    key_rows = lax.all_gather(rotary_keys, ("outer", "inner"), axis=0, tiled=True)
    val_rows = lax.all_gather(values, ("outer", "inner"), axis=0, tiled=True)

    def block_step(slot, state):
        key_block = lax.dynamic_slice_in_dim(key_rows, slot * TREE_BLOCK_SIZE, TREE_BLOCK_SIZE, 0)
        val_block = lax.dynamic_slice_in_dim(val_rows, slot * TREE_BLOCK_SIZE, TREE_BLOCK_SIZE, 0)
        return key_block_step(state, key_block, val_block, slot)

    running, total, weighted = lax.fori_loop(
        0, key_rows.shape[0] // TREE_BLOCK_SIZE, block_step, initial
    )
    attended = weighted / jnp.transpose(total, (2, 0, 1))[..., None]
    attended = attended.reshape(row_count, query_heads * HEAD_SIZE).astype(jnp.bfloat16)
    return lax.all_to_all(attended, "tensor", split_axis=0, concat_axis=1, tiled=True)


MESH = pl.DeviceIdType.MESH


def fused_kernel(
    outer_count, inner_count, tensor_count, listed,
    anc_ref, cut_ref, pos_ref, q_ref, k_ref, v_ref, out_ref,
    kv, turned, own_scores, staged, kv_send, kv_recv, out_send, out_recv,
):
    block_count = outer_count * inner_count
    width = q_ref.shape[1]
    heads = width // HEAD_SIZE
    chunk = TREE_BLOCK_SIZE // tensor_count
    rows = heads * chunk
    tensor_me = lax.axis_index("tensor")
    me = lax.axis_index("outer") * inner_count + lax.axis_index("inner")

    def block_device(j):
        return {"outer": j // inner_count, "inner": j % inner_count}

    def tensor_peer(step):
        return lax.rem(tensor_me + step, tensor_count)

    barrier = pltpu.get_barrier_semaphore()
    for step in range(1, tensor_count):
        pl.semaphore_signal(barrier, inc=1, device_id={"tensor": tensor_peer(step)}, device_id_type=MESH)
    for j in range(block_count - 1):
        @pl.when(j < me)
        def _():
            pl.semaphore_signal(barrier, inc=1, device_id=block_device(j), device_id_type=MESH)

    lane = lax.broadcasted_iota(jnp.int32, (TREE_BLOCK_SIZE, HEAD_SIZE), 1)
    row = lax.broadcasted_iota(jnp.int32, (TREE_BLOCK_SIZE, HEAD_SIZE), 0)
    half = HEAD_SIZE // 2
    pair = jnp.where(lane < half, lane, lane - half).astype(jnp.float32)
    frequency = jnp.exp(pair[:8] * ((-2.0 / HEAD_SIZE) * math.log(rope_base)))
    near = row[:8].astype(jnp.float32) * frequency
    near_cos, near_sin = jnp.cos(near), jnp.sin(near)
    tiles = TREE_BLOCK_SIZE // 8
    far_rows = (pos_ref[0] + 8 * row[:tiles]).astype(jnp.float32)
    far = far_rows * frequency[:1]
    far_cos, far_sin = jnp.cos(far), jnp.sin(far)
    cos_parts, sin_parts = [], []
    for tile in range(tiles):
        fc, fs = far_cos[tile : tile + 1], far_sin[tile : tile + 1]
        cos_parts.append(fc * near_cos - fs * near_sin)
        sin_parts.append(fs * near_cos + fc * near_sin)
    cosines = jnp.concatenate(cos_parts, axis=0)
    sines = jnp.concatenate(sin_parts, axis=0)
    sines = jnp.where(lane < half, -sines, sines)

    def rotate(x):
        x = x.astype(jnp.float32)
        return (x * cosines + pltpu.roll(x, half, 1) * sines).astype(jnp.bfloat16)

    own_keys = rotate(k_ref[...])
    kv[me, :TREE_BLOCK_SIZE] = own_keys
    kv[me, TREE_BLOCK_SIZE:] = v_ref[...]

    pl.semaphore_wait(barrier, tensor_count - 1 + block_count - 1 - me)

    def kv_copy(source, target, sem):
        return pltpu.make_async_remote_copy(
            src_ref=kv.at[source], dst_ref=kv.at[source],
            send_sem=kv_send.at[sem], recv_sem=kv_recv.at[source],
            device_id=block_device(target), device_id_type=MESH,
        )

    for j in range(1, block_count):
        @pl.when(j > me)
        def _():
            kv_copy(me, j, j).start()

    for head in range(heads):
        spun = rotate(q_ref[:, head * HEAD_SIZE : (head + 1) * HEAD_SIZE])
        for c in range(tensor_count):
            turned[c, head * chunk : (head + 1) * chunk] = spun[c * chunk : (c + 1) * chunk]
    row_in = lax.broadcasted_iota(jnp.int32, (rows, TREE_BLOCK_SIZE), 0) % chunk
    key_in = lax.broadcasted_iota(jnp.int32, (rows, TREE_BLOCK_SIZE), 1)
    contract_last = (((1,), (1,)), ((), ()))
    for c in range(tensor_count):
        s = lax.dot_general(turned[c], own_keys, contract_last, preferred_element_type=jnp.float32)
        own_scores[c] = jnp.where(key_in <= row_in + c * chunk, s, masked_low)

    for j in range(block_count - 1):
        @pl.when(j < me)
        def _():
            kv_copy(j, j, j).wait_recv()

    key_parts, val_parts, seen = [], [v_ref[...]], []
    for e in range(1, listed):
        index = jnp.maximum(anc_ref[0, e], 0)
        pair_block = kv[index]
        key_parts.append(pair_block[:TREE_BLOCK_SIZE])
        val_parts.append(pair_block[TREE_BLOCK_SIZE:])
        seen.append(key_in < cut_ref[0, e])
    far_keys = jnp.concatenate(key_parts, axis=0)
    all_vals = jnp.concatenate(val_parts, axis=0)
    factor = math.log2(math.e) / math.sqrt(HEAD_SIZE)

    def out_copy(step, column):
        return pltpu.make_async_remote_copy(
            src_ref=staged.at[step],
            dst_ref=out_ref.at[:, pl.ds(pl.multiple_of(column * width, width), width)],
            send_sem=out_send.at[step], recv_sem=out_recv.at[step],
            device_id={"tensor": tensor_peer(step)}, device_id_type=MESH,
        )

    for step in send_order(tensor_count):
        c = tensor_peer(step)
        s = lax.dot_general(turned[c], far_keys, contract_last, preferred_element_type=jnp.float32)
        parts = [own_scores[c]]
        for e in range(listed - 1):
            part = s[:, e * TREE_BLOCK_SIZE : (e + 1) * TREE_BLOCK_SIZE]
            parts.append(jnp.where(seen[e], part, masked_low))
        top = functools.reduce(jnp.maximum, parts)
        row_max = jnp.max(top, axis=1, keepdims=True)
        terms = [jnp.exp2((part - row_max) * factor) for part in parts]
        total = jnp.sum(functools.reduce(jnp.add, terms), axis=1, keepdims=True)
        weights = jnp.concatenate([t.astype(jnp.bfloat16) for t in terms], axis=1)
        summed = jnp.dot(weights, all_vals, preferred_element_type=jnp.float32)
        result = (summed / total).astype(jnp.bfloat16)
        for head in range(heads):
            piece = result[head * chunk : (head + 1) * chunk]
            if step == 0:
                column = tensor_me * width + head * HEAD_SIZE
                out_ref[:, pl.ds(pl.multiple_of(column, HEAD_SIZE), HEAD_SIZE)] = piece
            else:
                staged[step, :, head * HEAD_SIZE : (head + 1) * HEAD_SIZE] = piece
        if step != 0:
            out_copy(step, tensor_me).start()

    for j in range(1, block_count):
        @pl.when(j > me)
        def _():
            kv_copy(me, j, j).wait_send()
    for step in range(1, tensor_count):
        copy = out_copy(step, lax.rem(tensor_me + tensor_count - step, tensor_count))
        copy.wait_send()
        copy.wait_recv()


def send_order(tensor_count):
    return list(range(tensor_count - 1, -1, -1))


def fused(sizes, queries, keys, values, ancestors, visible_cut, positions):
    outer_count, inner_count, tensor_count = sizes
    block_count = outer_count * inner_count
    width = queries.shape[1]
    heads = width // HEAD_SIZE
    chunk = TREE_BLOCK_SIZE // tensor_count
    listed = ancestors.shape[1]
    vmem = pl.BlockSpec(memory_space=pltpu.VMEM)
    smem = pl.BlockSpec(memory_space=pltpu.SMEM)
    return pl.pallas_call(
        functools.partial(fused_kernel, outer_count, inner_count, tensor_count, listed),
        out_shape=jax.ShapeDtypeStruct((chunk, width * tensor_count), jnp.bfloat16),
        in_specs=[smem, smem, smem, vmem, vmem, vmem],
        out_specs=vmem,
        scratch_shapes=[
            pltpu.VMEM((block_count, 2 * TREE_BLOCK_SIZE, HEAD_SIZE), jnp.bfloat16),
            pltpu.VMEM((tensor_count, heads * chunk, HEAD_SIZE), jnp.bfloat16),
            pltpu.VMEM((tensor_count, heads * chunk, TREE_BLOCK_SIZE), jnp.float32),
            pltpu.VMEM((tensor_count, chunk, width), jnp.bfloat16),
            pltpu.SemaphoreType.DMA((block_count,)),
            pltpu.SemaphoreType.DMA((block_count,)),
            pltpu.SemaphoreType.DMA((tensor_count,)),
            pltpu.SemaphoreType.DMA((tensor_count,)),
        ],
        compiler_params=pltpu.CompilerParams(
            collective_id=0, has_side_effects=True, vmem_limit_bytes=32 * 1024 * 1024
        ),
    )(ancestors, visible_cut, positions, queries, keys, values)


def pick(sizes, queries, keys, *rest):
    small = (
        queries.shape[0] == TREE_BLOCK_SIZE
        and keys.shape[1] == HEAD_SIZE
        and sizes[0] * sizes[1] <= 16
        and rest[1].shape[1] <= 8
    )
    body = functools.partial(fused, sizes) if small else local
    return body(queries, keys, *rest)


def solution(mesh):
    placed = (
        P(("outer", "inner"), "tensor"),
        P(("outer", "inner"), "tensor"),
        P(("outer", "inner"), "tensor"),
        P(("outer", "inner"), None),
        P(("outer", "inner"), None),
        P(("outer", "inner")),
    )
    sizes = tuple(mesh.shape[name] for name in ("outer", "inner", "tensor"))
    return jax.shard_map(
        functools.partial(pick, sizes),
        mesh=mesh,
        in_specs=placed,
        out_specs=P(("outer", "inner", "tensor"), None),
        check_vma=False,
    )
```

```python
import functools
import math

import jax
import jax.numpy as jnp
from jax import lax
from jax.experimental import pallas as pl
from jax.experimental.pallas import tpu as pltpu
from jax.sharding import PartitionSpec as P

HEAD_SIZE = 128
TREE_BLOCK_SIZE = 128


rope_base = 500000.0
masked_low = -1e30


def apply_rotary(source, positions, head_count):
    token_count = source.shape[0]
    half_dim = HEAD_SIZE // 2
    frequency = jnp.exp(
        jnp.arange(half_dim, dtype=jnp.float32) * (-2.0 / HEAD_SIZE) * math.log(rope_base)
    )
    angles = positions.astype(jnp.float32)[:, None] * frequency[None, :]
    cosines = jnp.cos(angles)[:, None, :]
    sine_vals = jnp.sin(angles)[:, None, :]
    split_heads = source.astype(jnp.float32).reshape(token_count, head_count, HEAD_SIZE)
    front_half = split_heads[..., :half_dim]
    back_half = split_heads[..., half_dim:]
    turned = jnp.concatenate(
        [
            front_half * cosines - back_half * sine_vals,
            back_half * cosines + front_half * sine_vals,
        ],
        axis=-1,
    )
    return turned.reshape(token_count, head_count * HEAD_SIZE).astype(jnp.bfloat16)


def local(queries, keys, values, ancestors, visible_cut, positions):
    row_count = queries.shape[0]
    query_heads = queries.shape[1] // HEAD_SIZE
    kv_heads = keys.shape[1] // HEAD_SIZE
    head_group_width = query_heads // kv_heads
    scale = 1.0 / math.sqrt(HEAD_SIZE)
    rotary_queries = apply_rotary(queries, positions, query_heads)
    rotary_keys = apply_rotary(keys, positions, kv_heads)
    query_grid = rotary_queries.reshape(row_count, kv_heads, head_group_width, HEAD_SIZE)
    first_block = lax.axis_index(("outer", "inner")) * (row_count // TREE_BLOCK_SIZE)
    query_block = first_block + jnp.arange(row_count, dtype=jnp.int32) // TREE_BLOCK_SIZE
    query_inside = jnp.arange(row_count, dtype=jnp.int32) % TREE_BLOCK_SIZE
    key_inside = jnp.arange(TREE_BLOCK_SIZE, dtype=jnp.int32)

    def key_block_step(carried, key_block, val_block, key_id):
        cut_len = jnp.sum(jnp.where(ancestors == key_id, visible_cut, 0), axis=1)
        cut_rows = jnp.repeat(cut_len, TREE_BLOCK_SIZE)
        own_block = query_block == key_id
        visible = (key_inside[None, :] < cut_rows[:, None]) & (
            jnp.logical_not(own_block)[:, None] | (key_inside[None, :] <= query_inside[:, None])
        )

        def compute(state):
            running, total, weighted = state
            scores = (
                jnp.einsum(
                    "tkgd,skd->kgts",
                    query_grid,
                    key_block.reshape(TREE_BLOCK_SIZE, kv_heads, HEAD_SIZE),
                    preferred_element_type=jnp.float32,
                )
                * scale
            )
            scores = jnp.where(visible[None, None], scores, masked_low)
            new_max = jnp.maximum(running, jnp.max(scores, axis=-1))
            exp_terms = jnp.where(visible[None, None], jnp.exp(scores - new_max[..., None]), 0.0)
            rescale = jnp.exp(running - new_max)
            total = total * rescale + jnp.sum(exp_terms, axis=-1)
            weights = exp_terms.astype(jnp.bfloat16)
            update = jnp.einsum(
                "kgts,skd->tkgd",
                weights,
                val_block.reshape(TREE_BLOCK_SIZE, kv_heads, HEAD_SIZE),
                preferred_element_type=jnp.float32,
            )
            weighted = weighted * jnp.transpose(rescale, (2, 0, 1))[..., None] + update
            return (new_max, total, weighted)

        return lax.cond(jnp.any(visible), compute, lambda unchanged: unchanged, carried)

    initial = (
        jnp.full((kv_heads, head_group_width, row_count), masked_low, jnp.float32),
        jnp.zeros((kv_heads, head_group_width, row_count), jnp.float32),
        jnp.zeros((row_count, kv_heads, head_group_width, HEAD_SIZE), jnp.float32),
    )
    key_rows = lax.all_gather(rotary_keys, ("outer", "inner"), axis=0, tiled=True)
    val_rows = lax.all_gather(values, ("outer", "inner"), axis=0, tiled=True)

    def block_step(slot, state):
        key_block = lax.dynamic_slice_in_dim(key_rows, slot * TREE_BLOCK_SIZE, TREE_BLOCK_SIZE, 0)
        val_block = lax.dynamic_slice_in_dim(val_rows, slot * TREE_BLOCK_SIZE, TREE_BLOCK_SIZE, 0)
        return key_block_step(state, key_block, val_block, slot)

    running, total, weighted = lax.fori_loop(
        0, key_rows.shape[0] // TREE_BLOCK_SIZE, block_step, initial
    )
    attended = weighted / jnp.transpose(total, (2, 0, 1))[..., None]
    attended = attended.reshape(row_count, query_heads * HEAD_SIZE).astype(jnp.bfloat16)
    return lax.all_to_all(attended, "tensor", split_axis=0, concat_axis=1, tiled=True)


MESH = pl.DeviceIdType.MESH


def fused_kernel(
    outer_count, inner_count, tensor_count, listed,
    anc_hbm, cut_hbm, pos_hbm, q_hbm, k_hbm, v_hbm, out_ref,
    anc_ref, cut_ref, pos_ref, q_ref, k_ref,
    kv, turned, own_scores, staged, local_sem, kv_send, kv_pass, kv_recv, out_send, out_recv,
):
    block_count = outer_count * inner_count
    width = q_ref.shape[1]
    heads = width // HEAD_SIZE
    chunk = TREE_BLOCK_SIZE // tensor_count
    rows = heads * chunk
    tensor_me = lax.axis_index("tensor")
    outer_me = lax.axis_index("outer")
    inner_me = lax.axis_index("inner")
    me = outer_me * inner_count + inner_me
    chips = tensor_count // 2

    def tensor_peer(step):
        chip = lax.rem(tensor_me // 2 + step // 2, chips)
        return chip * 2 + lax.rem(lax.rem(tensor_me, 2) + step % 2, 2)

    def tensor_source(step):
        chip = lax.rem(tensor_me // 2 + chips - step // 2, chips)
        return chip * 2 + lax.rem(lax.rem(tensor_me, 2) + step % 2, 2)

    def load(i, source, target):
        return pltpu.make_async_copy(source, target, local_sem.at[i])

    loads = [
        load(0, pos_hbm, pos_ref),
        load(1, k_hbm, k_ref),
        load(2, v_hbm, kv.at[me, pl.ds(TREE_BLOCK_SIZE, TREE_BLOCK_SIZE)]),
        load(3, q_hbm, q_ref),
        load(4, anc_hbm, anc_ref),
        load(5, cut_hbm, cut_ref),
    ]
    for item in loads:
        item.start()

    def reaches(source_inner, target_inner):
        return (source_inner != target_inner) & ((outer_me == 0) | (source_inner < target_inner))

    barrier = pltpu.get_barrier_semaphore()
    for step in range(1, tensor_count):
        pl.semaphore_signal(barrier, inc=1, device_id={"tensor": tensor_peer(step)}, device_id_type=MESH)
    for z in range(inner_count):
        @pl.when(reaches(z, inner_me))
        def _():
            pl.semaphore_signal(barrier, inc=1, device_id={"inner": z}, device_id_type=MESH)
    @pl.when(outer_me == 1)
    def _():
        pl.semaphore_signal(barrier, inc=1, device_id={"outer": 0}, device_id_type=MESH)

    lane = lax.broadcasted_iota(jnp.int32, (TREE_BLOCK_SIZE, HEAD_SIZE), 1)
    row = lax.broadcasted_iota(jnp.int32, (TREE_BLOCK_SIZE, HEAD_SIZE), 0)
    half = HEAD_SIZE // 2
    pair = jnp.where(lane < half, lane, lane - half).astype(jnp.float32)
    frequency = jnp.exp(pair[:8] * ((-2.0 / HEAD_SIZE) * math.log(rope_base)))
    near = row[:8].astype(jnp.float32) * frequency
    near_cos, near_sin = jnp.cos(near), jnp.sin(near)
    tiles = TREE_BLOCK_SIZE // 8
    loads[0].wait()
    far_rows = (pos_ref[0] + 8 * row[:tiles]).astype(jnp.float32)
    far = far_rows * frequency[:1]
    far_cos, far_sin = jnp.cos(far), jnp.sin(far)
    cos_parts, sin_parts = [], []
    for tile in range(tiles):
        fc, fs = far_cos[tile : tile + 1], far_sin[tile : tile + 1]
        cos_parts.append(fc * near_cos - fs * near_sin)
        sin_parts.append(fs * near_cos + fc * near_sin)
    cosines = jnp.concatenate(cos_parts, axis=0)
    sines = jnp.concatenate(sin_parts, axis=0)
    sines = jnp.where(lane < half, -sines, sines)

    def rotate(x):
        x = x.astype(jnp.float32)
        return (x * cosines + pltpu.roll(x, half, 1) * sines).astype(jnp.bfloat16)

    loads[1].wait()
    own_keys = rotate(k_ref[...])
    kv[me, :TREE_BLOCK_SIZE] = own_keys
    loads[2].wait()

    sends = jnp.where(outer_me == 0, inner_count, inner_count - 1 - inner_me)
    pl.semaphore_wait(barrier, tensor_count - 1 + sends)

    def kv_copy(block, z):
        return pltpu.make_async_remote_copy(
            src_ref=kv.at[block], dst_ref=kv.at[block],
            send_sem=kv_send.at[z], recv_sem=kv_recv.at[block],
            device_id={"inner": z}, device_id_type=MESH,
        )

    def kv_forward(block):
        return pltpu.make_async_remote_copy(
            src_ref=kv.at[block], dst_ref=kv.at[block],
            send_sem=kv_pass.at[block], recv_sem=kv_recv.at[block],
            device_id={"outer": 1}, device_id_type=MESH,
        )

    @pl.when(outer_me == 0)
    def _():
        kv_forward(inner_me).start()
    for distance in range(inner_count - 1, 0, -1):
        for z in (inner_me - distance, inner_me + distance):
            @pl.when((z >= 0) & (z < inner_count) & reaches(inner_me, z))
            def _():
                kv_copy(me, z).start()

    def pass_on(distance):
        for z in (inner_me - distance, inner_me + distance):
            @pl.when((outer_me == 0) & (z >= 0) & (z < inner_count))
            def _():
                kv_copy(z, z).wait_recv()
                kv_forward(z).start()

    loads[3].wait()
    for head in range(heads):
        spun = rotate(q_ref[:, head * HEAD_SIZE : (head + 1) * HEAD_SIZE])
        for c in range(tensor_count):
            turned[c, head * chunk : (head + 1) * chunk] = spun[c * chunk : (c + 1) * chunk]
    for distance in range(1, inner_count):
        pass_on(distance)
    row_in = lax.broadcasted_iota(jnp.int32, (rows, TREE_BLOCK_SIZE), 0) % chunk
    key_in = lax.broadcasted_iota(jnp.int32, (rows, TREE_BLOCK_SIZE), 1)
    contract_last = (((1,), (1,)), ((), ()))
    for c in range(tensor_count):
        s = lax.dot_general(turned[c], own_keys, contract_last, preferred_element_type=jnp.float32)
        own_scores[c] = jnp.where(key_in <= row_in + c * chunk, s, masked_low)

    for j in range(block_count - 1):
        @pl.when((outer_me == 1) & (j < me))
        def _():
            kv_copy(j, inner_me).wait_recv()
    loads[4].wait()
    loads[5].wait()

    key_parts, val_parts, seen = [], [kv[me][TREE_BLOCK_SIZE:]], []
    for e in range(1, listed):
        index = jnp.maximum(anc_ref[0, e], 0)
        pair_block = kv[index]
        key_parts.append(pair_block[:TREE_BLOCK_SIZE])
        val_parts.append(pair_block[TREE_BLOCK_SIZE:])
        seen.append(key_in < cut_ref[0, e])
    far_keys = jnp.concatenate(key_parts, axis=0)
    all_vals = jnp.concatenate(val_parts, axis=0)
    factor = math.log2(math.e) / math.sqrt(HEAD_SIZE)

    def out_copy(step, column):
        return pltpu.make_async_remote_copy(
            src_ref=staged.at[step],
            dst_ref=out_ref.at[:, pl.ds(pl.multiple_of(column * width, width), width)],
            send_sem=out_send.at[step], recv_sem=out_recv.at[step],
            device_id={"tensor": tensor_peer(step)}, device_id_type=MESH,
        )

    for step in send_order(tensor_count):
        c = tensor_peer(step)
        s = lax.dot_general(turned[c], far_keys, contract_last, preferred_element_type=jnp.float32)
        parts = [own_scores[c]]
        for e in range(listed - 1):
            part = s[:, e * TREE_BLOCK_SIZE : (e + 1) * TREE_BLOCK_SIZE]
            parts.append(jnp.where(seen[e], part, masked_low))
        top = functools.reduce(jnp.maximum, parts)
        row_max = jnp.max(top, axis=1, keepdims=True)
        terms = [jnp.exp2((part - row_max) * factor) for part in parts]
        total = jnp.sum(functools.reduce(jnp.add, terms), axis=1, keepdims=True)
        weights = jnp.concatenate([t.astype(jnp.bfloat16) for t in terms], axis=1)
        summed = jnp.dot(weights, all_vals, preferred_element_type=jnp.float32)
        result = (summed / total).astype(jnp.bfloat16)
        for head in range(heads):
            piece = result[head * chunk : (head + 1) * chunk]
            if step == 0:
                column = tensor_me * width + head * HEAD_SIZE
                out_ref[:, pl.ds(pl.multiple_of(column, HEAD_SIZE), HEAD_SIZE)] = piece
            else:
                staged[step, :, head * HEAD_SIZE : (head + 1) * HEAD_SIZE] = piece
        if step != 0:
            out_copy(step, tensor_me).start()

    for z in range(inner_count):
        @pl.when(reaches(inner_me, z))
        def _():
            kv_copy(me, z).wait_send()
        @pl.when(outer_me == 0)
        def _():
            kv_forward(z).wait_send()
    for step in range(1, tensor_count):
        copy = out_copy(step, tensor_source(step))
        copy.wait_send()
        copy.wait_recv()


def send_order(tensor_count):
    return list(range(tensor_count - 1, -1, -1))


def fused(sizes, queries, keys, values, ancestors, visible_cut, positions):
    outer_count, inner_count, tensor_count = sizes
    block_count = outer_count * inner_count
    width = queries.shape[1]
    heads = width // HEAD_SIZE
    chunk = TREE_BLOCK_SIZE // tensor_count
    listed = ancestors.shape[1]
    hbm = pl.BlockSpec(memory_space=pltpu.HBM)
    return pl.pallas_call(
        functools.partial(fused_kernel, outer_count, inner_count, tensor_count, listed),
        out_shape=jax.ShapeDtypeStruct((chunk, width * tensor_count), jnp.bfloat16),
        in_specs=[hbm] * 6,
        out_specs=pl.BlockSpec(memory_space=pltpu.VMEM),
        scratch_shapes=[
            pltpu.SMEM(ancestors.shape, jnp.int32),
            pltpu.SMEM(visible_cut.shape, jnp.int32),
            pltpu.SMEM(positions.shape, jnp.int32),
            pltpu.VMEM(queries.shape, jnp.bfloat16),
            pltpu.VMEM(keys.shape, jnp.bfloat16),
            pltpu.VMEM((block_count, 2 * TREE_BLOCK_SIZE, HEAD_SIZE), jnp.bfloat16),
            pltpu.VMEM((tensor_count, heads * chunk, HEAD_SIZE), jnp.bfloat16),
            pltpu.VMEM((tensor_count, heads * chunk, TREE_BLOCK_SIZE), jnp.float32),
            pltpu.VMEM((tensor_count, chunk, width), jnp.bfloat16),
            pltpu.SemaphoreType.DMA((6,)),
            pltpu.SemaphoreType.DMA((inner_count,)),
            pltpu.SemaphoreType.DMA((inner_count,)),
            pltpu.SemaphoreType.DMA((block_count,)),
            pltpu.SemaphoreType.DMA((tensor_count,)),
            pltpu.SemaphoreType.DMA((tensor_count,)),
        ],
        compiler_params=pltpu.CompilerParams(
            collective_id=0, has_side_effects=True, vmem_limit_bytes=64 * 1024 * 1024
        ),
    )(ancestors, visible_cut, positions, queries, keys, values)


def pick(sizes, queries, keys, *rest):
    small = (
        queries.shape[0] == TREE_BLOCK_SIZE
        and keys.shape[1] == HEAD_SIZE
        and sizes[0] == 2
        and sizes[1] <= 8
        and sizes[2] % 2 == 0
        and rest[1].shape[1] <= 8
    )
    body = functools.partial(fused, sizes) if small else local
    return body(queries, keys, *rest)


def solution(mesh):
    placed = (
        P(("outer", "inner"), "tensor"),
        P(("outer", "inner"), "tensor"),
        P(("outer", "inner"), "tensor"),
        P(("outer", "inner"), None),
        P(("outer", "inner"), None),
        P(("outer", "inner")),
    )
    sizes = tuple(mesh.shape[name] for name in ("outer", "inner", "tensor"))
    return jax.shard_map(
        functools.partial(pick, sizes),
        mesh=mesh,
        in_specs=placed,
        out_specs=P(("outer", "inner", "tensor"), None),
        check_vma=False,
    )
```

```python
import functools
import math

import jax
import jax.numpy as jnp
from jax import lax
from jax.experimental import pallas as pl
from jax.experimental.pallas import tpu as pltpu
from jax.sharding import PartitionSpec as P

HEAD_SIZE = 128
TREE_BLOCK_SIZE = 128


rope_base = 500000.0
masked_low = -1e30


def apply_rotary(source, positions, head_count):
    token_count = source.shape[0]
    half_dim = HEAD_SIZE // 2
    frequency = jnp.exp(
        jnp.arange(half_dim, dtype=jnp.float32) * (-2.0 / HEAD_SIZE) * math.log(rope_base)
    )
    angles = positions.astype(jnp.float32)[:, None] * frequency[None, :]
    cosines = jnp.cos(angles)[:, None, :]
    sine_vals = jnp.sin(angles)[:, None, :]
    split_heads = source.astype(jnp.float32).reshape(token_count, head_count, HEAD_SIZE)
    front_half = split_heads[..., :half_dim]
    back_half = split_heads[..., half_dim:]
    turned = jnp.concatenate(
        [
            front_half * cosines - back_half * sine_vals,
            back_half * cosines + front_half * sine_vals,
        ],
        axis=-1,
    )
    return turned.reshape(token_count, head_count * HEAD_SIZE).astype(jnp.bfloat16)


def local(queries, keys, values, ancestors, visible_cut, positions):
    row_count = queries.shape[0]
    query_heads = queries.shape[1] // HEAD_SIZE
    kv_heads = keys.shape[1] // HEAD_SIZE
    head_group_width = query_heads // kv_heads
    scale = 1.0 / math.sqrt(HEAD_SIZE)
    rotary_queries = apply_rotary(queries, positions, query_heads)
    rotary_keys = apply_rotary(keys, positions, kv_heads)
    query_grid = rotary_queries.reshape(row_count, kv_heads, head_group_width, HEAD_SIZE)
    first_block = lax.axis_index(("outer", "inner")) * (row_count // TREE_BLOCK_SIZE)
    query_block = first_block + jnp.arange(row_count, dtype=jnp.int32) // TREE_BLOCK_SIZE
    query_inside = jnp.arange(row_count, dtype=jnp.int32) % TREE_BLOCK_SIZE
    key_inside = jnp.arange(TREE_BLOCK_SIZE, dtype=jnp.int32)

    def key_block_step(carried, key_block, val_block, key_id):
        cut_len = jnp.sum(jnp.where(ancestors == key_id, visible_cut, 0), axis=1)
        cut_rows = jnp.repeat(cut_len, TREE_BLOCK_SIZE)
        own_block = query_block == key_id
        visible = (key_inside[None, :] < cut_rows[:, None]) & (
            jnp.logical_not(own_block)[:, None] | (key_inside[None, :] <= query_inside[:, None])
        )

        def compute(state):
            running, total, weighted = state
            scores = (
                jnp.einsum(
                    "tkgd,skd->kgts",
                    query_grid,
                    key_block.reshape(TREE_BLOCK_SIZE, kv_heads, HEAD_SIZE),
                    preferred_element_type=jnp.float32,
                )
                * scale
            )
            scores = jnp.where(visible[None, None], scores, masked_low)
            new_max = jnp.maximum(running, jnp.max(scores, axis=-1))
            exp_terms = jnp.where(visible[None, None], jnp.exp(scores - new_max[..., None]), 0.0)
            rescale = jnp.exp(running - new_max)
            total = total * rescale + jnp.sum(exp_terms, axis=-1)
            weights = exp_terms.astype(jnp.bfloat16)
            update = jnp.einsum(
                "kgts,skd->tkgd",
                weights,
                val_block.reshape(TREE_BLOCK_SIZE, kv_heads, HEAD_SIZE),
                preferred_element_type=jnp.float32,
            )
            weighted = weighted * jnp.transpose(rescale, (2, 0, 1))[..., None] + update
            return (new_max, total, weighted)

        return lax.cond(jnp.any(visible), compute, lambda unchanged: unchanged, carried)

    initial = (
        jnp.full((kv_heads, head_group_width, row_count), masked_low, jnp.float32),
        jnp.zeros((kv_heads, head_group_width, row_count), jnp.float32),
        jnp.zeros((row_count, kv_heads, head_group_width, HEAD_SIZE), jnp.float32),
    )
    key_rows = lax.all_gather(rotary_keys, ("outer", "inner"), axis=0, tiled=True)
    val_rows = lax.all_gather(values, ("outer", "inner"), axis=0, tiled=True)

    def block_step(slot, state):
        key_block = lax.dynamic_slice_in_dim(key_rows, slot * TREE_BLOCK_SIZE, TREE_BLOCK_SIZE, 0)
        val_block = lax.dynamic_slice_in_dim(val_rows, slot * TREE_BLOCK_SIZE, TREE_BLOCK_SIZE, 0)
        return key_block_step(state, key_block, val_block, slot)

    running, total, weighted = lax.fori_loop(
        0, key_rows.shape[0] // TREE_BLOCK_SIZE, block_step, initial
    )
    attended = weighted / jnp.transpose(total, (2, 0, 1))[..., None]
    attended = attended.reshape(row_count, query_heads * HEAD_SIZE).astype(jnp.bfloat16)
    return lax.all_to_all(attended, "tensor", split_axis=0, concat_axis=1, tiled=True)


MESH = pl.DeviceIdType.MESH


def fused_kernel(
    outer_count, inner_count, tensor_count, listed,
    anc_hbm, cut_hbm, pos_hbm, q_hbm, k_hbm, v_hbm, out_ref,
    anc_ref, cut_ref, pos_ref, q_ref, k_ref,
    kv, turned, own_scores, staged, local_sem, kv_send, kv_pass, kv_recv, out_send, out_recv,
):
    block_count = outer_count * inner_count
    width = q_ref.shape[1]
    heads = width // HEAD_SIZE
    chunk = TREE_BLOCK_SIZE // tensor_count
    rows = heads * chunk
    tensor_me = lax.axis_index("tensor")
    outer_me = lax.axis_index("outer")
    inner_me = lax.axis_index("inner")
    me = outer_me * inner_count + inner_me
    chips = tensor_count // 2

    def tensor_peer(step):
        chip = lax.rem(tensor_me // 2 + step // 2, chips)
        return chip * 2 + lax.rem(lax.rem(tensor_me, 2) + step % 2, 2)

    def tensor_source(step):
        chip = lax.rem(tensor_me // 2 + chips - step // 2, chips)
        return chip * 2 + lax.rem(lax.rem(tensor_me, 2) + step % 2, 2)

    def load(i, source, target):
        return pltpu.make_async_copy(source, target, local_sem.at[i])

    loads = [
        load(0, pos_hbm, pos_ref),
        load(1, k_hbm, k_ref),
        load(2, v_hbm, kv.at[me, pl.ds(TREE_BLOCK_SIZE, TREE_BLOCK_SIZE)]),
        load(3, q_hbm, q_ref),
        load(4, anc_hbm, anc_ref),
        load(5, cut_hbm, cut_ref),
    ]
    for item in loads:
        item.start()

    def reaches(source_inner, target_inner):
        return source_inner < target_inner

    barrier = pltpu.get_barrier_semaphore()
    for step in range(1, tensor_count):
        pl.semaphore_signal(barrier, inc=1, device_id={"tensor": tensor_peer(step)}, device_id_type=MESH)
    for z in range(inner_count):
        @pl.when(reaches(z, inner_me))
        def _():
            pl.semaphore_signal(barrier, inc=1, device_id={"inner": z}, device_id_type=MESH)
    for z in range(inner_count):
        @pl.when((outer_me == 1) & (z >= inner_me))
        def _():
            pl.semaphore_signal(barrier, inc=1, device_id={"outer": 0, "inner": z}, device_id_type=MESH)

    lane = lax.broadcasted_iota(jnp.int32, (TREE_BLOCK_SIZE, HEAD_SIZE), 1)
    row = lax.broadcasted_iota(jnp.int32, (TREE_BLOCK_SIZE, HEAD_SIZE), 0)
    half = HEAD_SIZE // 2
    pair = jnp.where(lane < half, lane, lane - half).astype(jnp.float32)
    frequency = jnp.exp(pair[:8] * ((-2.0 / HEAD_SIZE) * math.log(rope_base)))
    near = row[:8].astype(jnp.float32) * frequency
    near_cos, near_sin = jnp.cos(near), jnp.sin(near)
    tiles = TREE_BLOCK_SIZE // 8
    loads[0].wait()
    far_rows = (pos_ref[0] + 8 * row[:tiles]).astype(jnp.float32)
    far = far_rows * frequency[:1]
    far_cos, far_sin = jnp.cos(far), jnp.sin(far)
    cos_parts, sin_parts = [], []
    for tile in range(tiles):
        fc, fs = far_cos[tile : tile + 1], far_sin[tile : tile + 1]
        cos_parts.append(fc * near_cos - fs * near_sin)
        sin_parts.append(fs * near_cos + fc * near_sin)
    cosines = jnp.concatenate(cos_parts, axis=0)
    sines = jnp.concatenate(sin_parts, axis=0)
    sines = jnp.where(lane < half, -sines, sines)

    def rotate(x):
        x = x.astype(jnp.float32)
        return (x * cosines + pltpu.roll(x, half, 1) * sines).astype(jnp.bfloat16)

    loads[1].wait()
    own_keys = rotate(k_ref[...])
    kv[me, :TREE_BLOCK_SIZE] = own_keys
    loads[2].wait()

    sends = jnp.where(outer_me == 0, inner_count, inner_count - 1 - inner_me)
    pl.semaphore_wait(barrier, tensor_count - 1 + sends)

    def kv_copy(block, z):
        return pltpu.make_async_remote_copy(
            src_ref=kv.at[block], dst_ref=kv.at[block],
            send_sem=kv_send.at[z], recv_sem=kv_recv.at[block],
            device_id={"inner": z}, device_id_type=MESH,
        )

    def kv_down(z):
        return pltpu.make_async_remote_copy(
            src_ref=kv.at[me], dst_ref=kv.at[me],
            send_sem=kv_send.at[z], recv_sem=kv_recv.at[me],
            device_id={"outer": 1, "inner": z}, device_id_type=MESH,
        )

    def kv_forward(block):
        return pltpu.make_async_remote_copy(
            src_ref=kv.at[block], dst_ref=kv.at[block],
            send_sem=kv_pass.at[block], recv_sem=kv_recv.at[block],
            device_id={"outer": 1}, device_id_type=MESH,
        )

    @pl.when(outer_me == 0)
    def _():
        kv_forward(inner_me).start()
    for distance in range(1, inner_count):
        @pl.when(inner_me + distance < inner_count)
        def _():
            kv_copy(me, inner_me + distance).start()
        @pl.when((outer_me == 0) & (inner_me - distance >= 0))
        def _():
            kv_down(inner_me - distance).start()

    def pass_on(distance):
        z = inner_me - distance
        @pl.when((outer_me == 0) & (z >= 0))
        def _():
            kv_copy(z, z).wait_recv()
            kv_forward(z).start()

    loads[3].wait()
    for head in range(heads):
        spun = rotate(q_ref[:, head * HEAD_SIZE : (head + 1) * HEAD_SIZE])
        for c in range(tensor_count):
            turned[c, head * chunk : (head + 1) * chunk] = spun[c * chunk : (c + 1) * chunk]
    for distance in range(1, inner_count):
        pass_on(distance)
    row_in = lax.broadcasted_iota(jnp.int32, (rows, TREE_BLOCK_SIZE), 0) % chunk
    key_in = lax.broadcasted_iota(jnp.int32, (rows, TREE_BLOCK_SIZE), 1)
    contract_last = (((1,), (1,)), ((), ()))
    for c in range(tensor_count):
        s = lax.dot_general(turned[c], own_keys, contract_last, preferred_element_type=jnp.float32)
        own_scores[c] = jnp.where(key_in <= row_in + c * chunk, s, masked_low)

    for j in range(block_count - 1):
        @pl.when((outer_me == 1) & (j < me))
        def _():
            kv_copy(j, inner_me).wait_recv()
    loads[4].wait()
    loads[5].wait()

    key_parts, val_parts, seen = [], [kv[me][TREE_BLOCK_SIZE:]], []
    for e in range(1, listed):
        index = jnp.maximum(anc_ref[0, e], 0)
        pair_block = kv[index]
        key_parts.append(pair_block[:TREE_BLOCK_SIZE])
        val_parts.append(pair_block[TREE_BLOCK_SIZE:])
        seen.append(key_in < cut_ref[0, e])
    far_keys = jnp.concatenate(key_parts, axis=0)
    all_vals = jnp.concatenate(val_parts, axis=0)
    factor = math.log2(math.e) / math.sqrt(HEAD_SIZE)

    def out_copy(step, column):
        return pltpu.make_async_remote_copy(
            src_ref=staged.at[step],
            dst_ref=out_ref.at[:, pl.ds(pl.multiple_of(column * width, width), width)],
            send_sem=out_send.at[step], recv_sem=out_recv.at[step],
            device_id={"tensor": tensor_peer(step)}, device_id_type=MESH,
        )

    for step in send_order(tensor_count):
        c = tensor_peer(step)
        s = lax.dot_general(turned[c], far_keys, contract_last, preferred_element_type=jnp.float32)
        parts = [own_scores[c]]
        for e in range(listed - 1):
            part = s[:, e * TREE_BLOCK_SIZE : (e + 1) * TREE_BLOCK_SIZE]
            parts.append(jnp.where(seen[e], part, masked_low))
        top = functools.reduce(jnp.maximum, parts)
        row_max = jnp.max(top, axis=1, keepdims=True)
        terms = [jnp.exp2((part - row_max) * factor) for part in parts]
        total = jnp.sum(functools.reduce(jnp.add, terms), axis=1, keepdims=True)
        weights = jnp.concatenate([t.astype(jnp.bfloat16) for t in terms], axis=1)
        summed = jnp.dot(weights, all_vals, preferred_element_type=jnp.float32)
        result = (summed / total).astype(jnp.bfloat16)
        for head in range(heads):
            piece = result[head * chunk : (head + 1) * chunk]
            if step == 0:
                column = tensor_me * width + head * HEAD_SIZE
                out_ref[:, pl.ds(pl.multiple_of(column, HEAD_SIZE), HEAD_SIZE)] = piece
            else:
                staged[step, :, head * HEAD_SIZE : (head + 1) * HEAD_SIZE] = piece
        if step != 0:
            out_copy(step, tensor_me).start()

    for z in range(inner_count):
        @pl.when(reaches(inner_me, z))
        def _():
            kv_copy(me, z).wait_send()
        @pl.when((outer_me == 0) & (z < inner_me))
        def _():
            kv_down(z).wait_send()
        @pl.when((outer_me == 0) & (z <= inner_me))
        def _():
            kv_forward(z).wait_send()
    for step in range(1, tensor_count):
        copy = out_copy(step, tensor_source(step))
        copy.wait_send()
        copy.wait_recv()


def send_order(tensor_count):
    return list(range(tensor_count - 1, -1, -1))


def fused(sizes, queries, keys, values, ancestors, visible_cut, positions):
    outer_count, inner_count, tensor_count = sizes
    block_count = outer_count * inner_count
    width = queries.shape[1]
    heads = width // HEAD_SIZE
    chunk = TREE_BLOCK_SIZE // tensor_count
    listed = ancestors.shape[1]
    hbm = pl.BlockSpec(memory_space=pltpu.HBM)
    return pl.pallas_call(
        functools.partial(fused_kernel, outer_count, inner_count, tensor_count, listed),
        out_shape=jax.ShapeDtypeStruct((chunk, width * tensor_count), jnp.bfloat16),
        in_specs=[hbm] * 6,
        out_specs=pl.BlockSpec(memory_space=pltpu.VMEM),
        scratch_shapes=[
            pltpu.SMEM(ancestors.shape, jnp.int32),
            pltpu.SMEM(visible_cut.shape, jnp.int32),
            pltpu.SMEM(positions.shape, jnp.int32),
            pltpu.VMEM(queries.shape, jnp.bfloat16),
            pltpu.VMEM(keys.shape, jnp.bfloat16),
            pltpu.VMEM((block_count, 2 * TREE_BLOCK_SIZE, HEAD_SIZE), jnp.bfloat16),
            pltpu.VMEM((tensor_count, heads * chunk, HEAD_SIZE), jnp.bfloat16),
            pltpu.VMEM((tensor_count, heads * chunk, TREE_BLOCK_SIZE), jnp.float32),
            pltpu.VMEM((tensor_count, chunk, width), jnp.bfloat16),
            pltpu.SemaphoreType.DMA((6,)),
            pltpu.SemaphoreType.DMA((inner_count,)),
            pltpu.SemaphoreType.DMA((inner_count,)),
            pltpu.SemaphoreType.DMA((block_count,)),
            pltpu.SemaphoreType.DMA((tensor_count,)),
            pltpu.SemaphoreType.DMA((tensor_count,)),
        ],
        compiler_params=pltpu.CompilerParams(
            collective_id=0, has_side_effects=True, vmem_limit_bytes=64 * 1024 * 1024
        ),
    )(ancestors, visible_cut, positions, queries, keys, values)


def pick(sizes, queries, keys, *rest):
    small = (
        queries.shape[0] == TREE_BLOCK_SIZE
        and keys.shape[1] == HEAD_SIZE
        and sizes[0] == 2
        and sizes[1] <= 8
        and sizes[2] % 2 == 0
        and rest[1].shape[1] <= 8
    )
    body = functools.partial(fused, sizes) if small else local
    return body(queries, keys, *rest)


def solution(mesh):
    placed = (
        P(("outer", "inner"), "tensor"),
        P(("outer", "inner"), "tensor"),
        P(("outer", "inner"), "tensor"),
        P(("outer", "inner"), None),
        P(("outer", "inner"), None),
        P(("outer", "inner")),
    )
    sizes = tuple(mesh.shape[name] for name in ("outer", "inner", "tensor"))
    return jax.shard_map(
        functools.partial(pick, sizes),
        mesh=mesh,
        in_specs=placed,
        out_specs=P(("outer", "inner", "tensor"), None),
        check_vma=False,
    )
```

```python
import functools
import math

import jax
import jax.numpy as jnp
from jax import lax
from jax.experimental import pallas as pl
from jax.experimental.pallas import tpu as pltpu
from jax.sharding import PartitionSpec as P

HEAD_SIZE = 128
TREE_BLOCK_SIZE = 128


rope_base = 500000.0
masked_low = -1e30


def apply_rotary(source, positions, head_count):
    token_count = source.shape[0]
    half_dim = HEAD_SIZE // 2
    frequency = jnp.exp(
        jnp.arange(half_dim, dtype=jnp.float32) * (-2.0 / HEAD_SIZE) * math.log(rope_base)
    )
    angles = positions.astype(jnp.float32)[:, None] * frequency[None, :]
    cosines = jnp.cos(angles)[:, None, :]
    sine_vals = jnp.sin(angles)[:, None, :]
    split_heads = source.astype(jnp.float32).reshape(token_count, head_count, HEAD_SIZE)
    front_half = split_heads[..., :half_dim]
    back_half = split_heads[..., half_dim:]
    turned = jnp.concatenate(
        [
            front_half * cosines - back_half * sine_vals,
            back_half * cosines + front_half * sine_vals,
        ],
        axis=-1,
    )
    return turned.reshape(token_count, head_count * HEAD_SIZE).astype(jnp.bfloat16)


def local(queries, keys, values, ancestors, visible_cut, positions):
    row_count = queries.shape[0]
    query_heads = queries.shape[1] // HEAD_SIZE
    kv_heads = keys.shape[1] // HEAD_SIZE
    head_group_width = query_heads // kv_heads
    scale = 1.0 / math.sqrt(HEAD_SIZE)
    rotary_queries = apply_rotary(queries, positions, query_heads)
    rotary_keys = apply_rotary(keys, positions, kv_heads)
    query_grid = rotary_queries.reshape(row_count, kv_heads, head_group_width, HEAD_SIZE)
    first_block = lax.axis_index(("outer", "inner")) * (row_count // TREE_BLOCK_SIZE)
    query_block = first_block + jnp.arange(row_count, dtype=jnp.int32) // TREE_BLOCK_SIZE
    query_inside = jnp.arange(row_count, dtype=jnp.int32) % TREE_BLOCK_SIZE
    key_inside = jnp.arange(TREE_BLOCK_SIZE, dtype=jnp.int32)

    def key_block_step(carried, key_block, val_block, key_id):
        cut_len = jnp.sum(jnp.where(ancestors == key_id, visible_cut, 0), axis=1)
        cut_rows = jnp.repeat(cut_len, TREE_BLOCK_SIZE)
        own_block = query_block == key_id
        visible = (key_inside[None, :] < cut_rows[:, None]) & (
            jnp.logical_not(own_block)[:, None] | (key_inside[None, :] <= query_inside[:, None])
        )

        def compute(state):
            running, total, weighted = state
            scores = (
                jnp.einsum(
                    "tkgd,skd->kgts",
                    query_grid,
                    key_block.reshape(TREE_BLOCK_SIZE, kv_heads, HEAD_SIZE),
                    preferred_element_type=jnp.float32,
                )
                * scale
            )
            scores = jnp.where(visible[None, None], scores, masked_low)
            new_max = jnp.maximum(running, jnp.max(scores, axis=-1))
            exp_terms = jnp.where(visible[None, None], jnp.exp(scores - new_max[..., None]), 0.0)
            rescale = jnp.exp(running - new_max)
            total = total * rescale + jnp.sum(exp_terms, axis=-1)
            weights = exp_terms.astype(jnp.bfloat16)
            update = jnp.einsum(
                "kgts,skd->tkgd",
                weights,
                val_block.reshape(TREE_BLOCK_SIZE, kv_heads, HEAD_SIZE),
                preferred_element_type=jnp.float32,
            )
            weighted = weighted * jnp.transpose(rescale, (2, 0, 1))[..., None] + update
            return (new_max, total, weighted)

        return lax.cond(jnp.any(visible), compute, lambda unchanged: unchanged, carried)

    initial = (
        jnp.full((kv_heads, head_group_width, row_count), masked_low, jnp.float32),
        jnp.zeros((kv_heads, head_group_width, row_count), jnp.float32),
        jnp.zeros((row_count, kv_heads, head_group_width, HEAD_SIZE), jnp.float32),
    )
    key_rows = lax.all_gather(rotary_keys, ("outer", "inner"), axis=0, tiled=True)
    val_rows = lax.all_gather(values, ("outer", "inner"), axis=0, tiled=True)

    def block_step(slot, state):
        key_block = lax.dynamic_slice_in_dim(key_rows, slot * TREE_BLOCK_SIZE, TREE_BLOCK_SIZE, 0)
        val_block = lax.dynamic_slice_in_dim(val_rows, slot * TREE_BLOCK_SIZE, TREE_BLOCK_SIZE, 0)
        return key_block_step(state, key_block, val_block, slot)

    running, total, weighted = lax.fori_loop(
        0, key_rows.shape[0] // TREE_BLOCK_SIZE, block_step, initial
    )
    attended = weighted / jnp.transpose(total, (2, 0, 1))[..., None]
    attended = attended.reshape(row_count, query_heads * HEAD_SIZE).astype(jnp.bfloat16)
    return lax.all_to_all(attended, "tensor", split_axis=0, concat_axis=1, tiled=True)


MESH = pl.DeviceIdType.MESH


def fused_kernel(
    outer_count, inner_count, tensor_count, listed,
    anc_hbm, cut_hbm, pos_hbm, q_hbm, k_hbm, v_hbm, out_ref,
    anc_ref, cut_ref, pos_ref, q_ref, k_ref,
    kv, turned, own_scores, staged, local_sem, kv_send, kv_pass, kv_recv, out_send, out_recv,
):
    block_count = outer_count * inner_count
    width = q_ref.shape[1]
    heads = width // HEAD_SIZE
    chunk = TREE_BLOCK_SIZE // tensor_count
    rows = heads * chunk
    tensor_me = lax.axis_index("tensor")
    outer_me = lax.axis_index("outer")
    inner_me = lax.axis_index("inner")
    me = outer_me * inner_count + inner_me
    chips = tensor_count // 2

    def tensor_peer(step):
        chip = lax.rem(tensor_me // 2 + step // 2, chips)
        return chip * 2 + lax.rem(lax.rem(tensor_me, 2) + step % 2, 2)

    def tensor_source(step):
        chip = lax.rem(tensor_me // 2 + chips - step // 2, chips)
        return chip * 2 + lax.rem(lax.rem(tensor_me, 2) + step % 2, 2)

    def load(i, source, target):
        return pltpu.make_async_copy(source, target, local_sem.at[i])

    loads = [
        load(0, pos_hbm, pos_ref),
        load(1, k_hbm, k_ref),
        load(2, v_hbm, kv.at[me, pl.ds(TREE_BLOCK_SIZE, TREE_BLOCK_SIZE)]),
        load(3, q_hbm, q_ref),
        load(4, anc_hbm, anc_ref),
        load(5, cut_hbm, cut_ref),
    ]
    for item in loads:
        item.start()

    def reaches(source_inner, target_inner):
        relayed = (lax.rem(source_inner, 2) == 1) & (target_inner - source_inner == 2)
        return (source_inner < target_inner) & jnp.logical_not(relayed)

    barrier = pltpu.get_barrier_semaphore()
    for step in range(1, tensor_count):
        pl.semaphore_signal(barrier, inc=1, device_id={"tensor": tensor_peer(step)}, device_id_type=MESH)
    for z in range(inner_count):
        @pl.when(reaches(z, inner_me))
        def _():
            pl.semaphore_signal(barrier, inc=1, device_id={"inner": z}, device_id_type=MESH)
    for z in range(inner_count):
        @pl.when((outer_me == 1) & (z >= inner_me))
        def _():
            pl.semaphore_signal(barrier, inc=1, device_id={"outer": 0, "inner": z}, device_id_type=MESH)

    lane = lax.broadcasted_iota(jnp.int32, (TREE_BLOCK_SIZE, HEAD_SIZE), 1)
    row = lax.broadcasted_iota(jnp.int32, (TREE_BLOCK_SIZE, HEAD_SIZE), 0)
    half = HEAD_SIZE // 2
    pair = jnp.where(lane < half, lane, lane - half).astype(jnp.float32)
    frequency = jnp.exp(pair[:8] * ((-2.0 / HEAD_SIZE) * math.log(rope_base)))
    near = row[:8].astype(jnp.float32) * frequency
    near_cos, near_sin = jnp.cos(near), jnp.sin(near)
    tiles = TREE_BLOCK_SIZE // 8
    loads[0].wait()
    far_rows = (pos_ref[0] + 8 * row[:tiles]).astype(jnp.float32)
    far = far_rows * frequency[:1]
    far_cos, far_sin = jnp.cos(far), jnp.sin(far)
    cos_parts, sin_parts = [], []
    for tile in range(tiles):
        fc, fs = far_cos[tile : tile + 1], far_sin[tile : tile + 1]
        cos_parts.append(fc * near_cos - fs * near_sin)
        sin_parts.append(fs * near_cos + fc * near_sin)
    cosines = jnp.concatenate(cos_parts, axis=0)
    sines = jnp.concatenate(sin_parts, axis=0)
    sines = jnp.where(lane < half, -sines, sines)

    def rotate(x):
        x = x.astype(jnp.float32)
        return (x * cosines + pltpu.roll(x, half, 1) * sines).astype(jnp.bfloat16)

    loads[1].wait()
    own_keys = rotate(k_ref[...])
    kv[me, :TREE_BLOCK_SIZE] = own_keys
    loads[2].wait()

    sends = inner_count - 1 - inner_me + jnp.where(outer_me == 0, inner_me + 1, 0)
    inner_odd = lax.rem(inner_me, 2) == 1
    relays = jnp.logical_not(inner_odd) & (inner_me >= 2) & (inner_me + 1 < inner_count)
    skips = jnp.where(inner_odd & (inner_me + 2 < inner_count), 1, 0)
    pl.semaphore_wait(barrier, tensor_count - 1 + sends - skips)

    def kv_copy(block, z):
        return pltpu.make_async_remote_copy(
            src_ref=kv.at[block], dst_ref=kv.at[block],
            send_sem=kv_send.at[z], recv_sem=kv_recv.at[block],
            device_id={"inner": z}, device_id_type=MESH,
        )

    def kv_down(z):
        return pltpu.make_async_remote_copy(
            src_ref=kv.at[me], dst_ref=kv.at[me],
            send_sem=kv_send.at[z], recv_sem=kv_recv.at[me],
            device_id={"outer": 1, "inner": z}, device_id_type=MESH,
        )

    def kv_forward(block):
        return pltpu.make_async_remote_copy(
            src_ref=kv.at[block], dst_ref=kv.at[block],
            send_sem=kv_pass.at[block], recv_sem=kv_recv.at[block],
            device_id={"outer": 1}, device_id_type=MESH,
        )

    @pl.when(outer_me == 0)
    def _():
        kv_forward(inner_me).start()
    for distance in range(1, inner_count):
        @pl.when((inner_me + distance < inner_count) & reaches(inner_me, inner_me + distance))
        def _():
            kv_copy(me, inner_me + distance).start()
        @pl.when((outer_me == 0) & (inner_me - distance >= 0))
        def _():
            kv_down(inner_me - distance).start()

    def kv_relay():
        return pltpu.make_async_remote_copy(
            src_ref=kv.at[me - 1], dst_ref=kv.at[me - 1],
            send_sem=kv_pass.at[inner_me + 1], recv_sem=kv_recv.at[me - 1],
            device_id={"inner": inner_me + 1}, device_id_type=MESH,
        )

    def pass_on(distance):
        z = inner_me - distance
        @pl.when((outer_me == 0) & (z >= 0))
        def _():
            kv_copy(z, z).wait_recv()
            if distance == 1:
                @pl.when(relays)
                def _():
                    kv_relay().start()
            kv_forward(z).start()
        if distance == 1:
            @pl.when((outer_me == 1) & relays)
            def _():
                kv_relay().wait_recv()
                kv_relay().start()

    loads[3].wait()
    for head in range(heads):
        spun = rotate(q_ref[:, head * HEAD_SIZE : (head + 1) * HEAD_SIZE])
        for c in range(tensor_count):
            turned[c, head * chunk : (head + 1) * chunk] = spun[c * chunk : (c + 1) * chunk]
    for distance in range(1, inner_count):
        pass_on(distance)
    row_in = lax.broadcasted_iota(jnp.int32, (rows, TREE_BLOCK_SIZE), 0) % chunk
    key_in = lax.broadcasted_iota(jnp.int32, (rows, TREE_BLOCK_SIZE), 1)
    contract_last = (((1,), (1,)), ((), ()))
    for c in range(tensor_count):
        s = lax.dot_general(turned[c], own_keys, contract_last, preferred_element_type=jnp.float32)
        own_scores[c] = jnp.where(key_in <= row_in + c * chunk, s, masked_low)

    for j in range(block_count - 1):
        @pl.when((outer_me == 1) & (j < me) & jnp.logical_not(relays & (j == me - 1)))
        def _():
            kv_copy(j, inner_me).wait_recv()
    loads[4].wait()
    loads[5].wait()

    key_parts, val_parts, seen = [], [kv[me][TREE_BLOCK_SIZE:]], []
    for e in range(1, listed):
        index = jnp.maximum(anc_ref[0, e], 0)
        pair_block = kv[index]
        key_parts.append(pair_block[:TREE_BLOCK_SIZE])
        val_parts.append(pair_block[TREE_BLOCK_SIZE:])
        seen.append(key_in < cut_ref[0, e])
    far_keys = jnp.concatenate(key_parts, axis=0)
    all_vals = jnp.concatenate(val_parts, axis=0)
    factor = math.log2(math.e) / math.sqrt(HEAD_SIZE)

    def out_copy(step, column):
        return pltpu.make_async_remote_copy(
            src_ref=staged.at[step],
            dst_ref=out_ref.at[:, pl.ds(pl.multiple_of(column * width, width), width)],
            send_sem=out_send.at[step], recv_sem=out_recv.at[step],
            device_id={"tensor": tensor_peer(step)}, device_id_type=MESH,
        )

    for step in send_order(tensor_count):
        c = tensor_peer(step)
        s = lax.dot_general(turned[c], far_keys, contract_last, preferred_element_type=jnp.float32)
        parts = [own_scores[c]]
        for e in range(listed - 1):
            part = s[:, e * TREE_BLOCK_SIZE : (e + 1) * TREE_BLOCK_SIZE]
            parts.append(jnp.where(seen[e], part, masked_low))
        top = functools.reduce(jnp.maximum, parts)
        row_max = jnp.max(top, axis=1, keepdims=True)
        terms = [jnp.exp2((part - row_max) * factor) for part in parts]
        total = jnp.sum(functools.reduce(jnp.add, terms), axis=1, keepdims=True)
        weights = jnp.concatenate([t.astype(jnp.bfloat16) for t in terms], axis=1)
        summed = jnp.dot(weights, all_vals, preferred_element_type=jnp.float32)
        result = (summed / total).astype(jnp.bfloat16)
        for head in range(heads):
            piece = result[head * chunk : (head + 1) * chunk]
            if step == 0:
                column = tensor_me * width + head * HEAD_SIZE
                out_ref[:, pl.ds(pl.multiple_of(column, HEAD_SIZE), HEAD_SIZE)] = piece
            else:
                staged[step, :, head * HEAD_SIZE : (head + 1) * HEAD_SIZE] = piece
        if step != 0:
            out_copy(step, tensor_me).start()

    for z in range(inner_count):
        @pl.when(reaches(inner_me, z))
        def _():
            kv_copy(me, z).wait_send()
        @pl.when((outer_me == 0) & (z < inner_me))
        def _():
            kv_down(z).wait_send()
        @pl.when((outer_me == 0) & (z <= inner_me))
        def _():
            kv_forward(z).wait_send()
    @pl.when(relays)
    def _():
        kv_relay().wait_send()
    for step in range(1, tensor_count):
        copy = out_copy(step, tensor_source(step))
        copy.wait_send()
        copy.wait_recv()


def send_order(tensor_count):
    return list(range(tensor_count - 1, -1, -1))


def fused(sizes, queries, keys, values, ancestors, visible_cut, positions):
    outer_count, inner_count, tensor_count = sizes
    block_count = outer_count * inner_count
    width = queries.shape[1]
    heads = width // HEAD_SIZE
    chunk = TREE_BLOCK_SIZE // tensor_count
    listed = ancestors.shape[1]
    hbm = pl.BlockSpec(memory_space=pltpu.HBM)
    return pl.pallas_call(
        functools.partial(fused_kernel, outer_count, inner_count, tensor_count, listed),
        out_shape=jax.ShapeDtypeStruct((chunk, width * tensor_count), jnp.bfloat16),
        in_specs=[hbm] * 6,
        out_specs=pl.BlockSpec(memory_space=pltpu.VMEM),
        scratch_shapes=[
            pltpu.SMEM(ancestors.shape, jnp.int32),
            pltpu.SMEM(visible_cut.shape, jnp.int32),
            pltpu.SMEM(positions.shape, jnp.int32),
            pltpu.VMEM(queries.shape, jnp.bfloat16),
            pltpu.VMEM(keys.shape, jnp.bfloat16),
            pltpu.VMEM((block_count, 2 * TREE_BLOCK_SIZE, HEAD_SIZE), jnp.bfloat16),
            pltpu.VMEM((tensor_count, heads * chunk, HEAD_SIZE), jnp.bfloat16),
            pltpu.VMEM((tensor_count, heads * chunk, TREE_BLOCK_SIZE), jnp.float32),
            pltpu.VMEM((tensor_count, chunk, width), jnp.bfloat16),
            pltpu.SemaphoreType.DMA((6,)),
            pltpu.SemaphoreType.DMA((inner_count,)),
            pltpu.SemaphoreType.DMA((inner_count,)),
            pltpu.SemaphoreType.DMA((block_count,)),
            pltpu.SemaphoreType.DMA((tensor_count,)),
            pltpu.SemaphoreType.DMA((tensor_count,)),
        ],
        compiler_params=pltpu.CompilerParams(
            collective_id=0, has_side_effects=True, vmem_limit_bytes=64 * 1024 * 1024
        ),
    )(ancestors, visible_cut, positions, queries, keys, values)


def pick(sizes, queries, keys, *rest):
    small = (
        queries.shape[0] == TREE_BLOCK_SIZE
        and keys.shape[1] == HEAD_SIZE
        and sizes[0] == 2
        and sizes[1] <= 8
        and sizes[2] % 2 == 0
        and rest[1].shape[1] <= 8
    )
    body = functools.partial(fused, sizes) if small else local
    return body(queries, keys, *rest)


def solution(mesh):
    placed = (
        P(("outer", "inner"), "tensor"),
        P(("outer", "inner"), "tensor"),
        P(("outer", "inner"), "tensor"),
        P(("outer", "inner"), None),
        P(("outer", "inner"), None),
        P(("outer", "inner")),
    )
    sizes = tuple(mesh.shape[name] for name in ("outer", "inner", "tensor"))
    return jax.shard_map(
        functools.partial(pick, sizes),
        mesh=mesh,
        in_specs=placed,
        out_specs=P(("outer", "inner", "tensor"), None),
        check_vma=False,
    )
```

```python
import functools
import math

import jax
import jax.numpy as jnp
from jax import lax
from jax.experimental import pallas as pl
from jax.experimental.pallas import tpu as pltpu
from jax.sharding import PartitionSpec as P

HEAD_SIZE = 128
TREE_BLOCK_SIZE = 128


rope_base = 500000.0
masked_low = -1e30


def apply_rotary(source, positions, head_count):
    token_count = source.shape[0]
    half_dim = HEAD_SIZE // 2
    frequency = jnp.exp(
        jnp.arange(half_dim, dtype=jnp.float32) * (-2.0 / HEAD_SIZE) * math.log(rope_base)
    )
    angles = positions.astype(jnp.float32)[:, None] * frequency[None, :]
    cosines = jnp.cos(angles)[:, None, :]
    sine_vals = jnp.sin(angles)[:, None, :]
    split_heads = source.astype(jnp.float32).reshape(token_count, head_count, HEAD_SIZE)
    front_half = split_heads[..., :half_dim]
    back_half = split_heads[..., half_dim:]
    turned = jnp.concatenate(
        [
            front_half * cosines - back_half * sine_vals,
            back_half * cosines + front_half * sine_vals,
        ],
        axis=-1,
    )
    return turned.reshape(token_count, head_count * HEAD_SIZE).astype(jnp.bfloat16)


def local(queries, keys, values, ancestors, visible_cut, positions):
    row_count = queries.shape[0]
    query_heads = queries.shape[1] // HEAD_SIZE
    kv_heads = keys.shape[1] // HEAD_SIZE
    head_group_width = query_heads // kv_heads
    scale = 1.0 / math.sqrt(HEAD_SIZE)
    rotary_queries = apply_rotary(queries, positions, query_heads)
    rotary_keys = apply_rotary(keys, positions, kv_heads)
    query_grid = rotary_queries.reshape(row_count, kv_heads, head_group_width, HEAD_SIZE)
    first_block = lax.axis_index(("outer", "inner")) * (row_count // TREE_BLOCK_SIZE)
    query_block = first_block + jnp.arange(row_count, dtype=jnp.int32) // TREE_BLOCK_SIZE
    query_inside = jnp.arange(row_count, dtype=jnp.int32) % TREE_BLOCK_SIZE
    key_inside = jnp.arange(TREE_BLOCK_SIZE, dtype=jnp.int32)

    def key_block_step(carried, key_block, val_block, key_id):
        cut_len = jnp.sum(jnp.where(ancestors == key_id, visible_cut, 0), axis=1)
        cut_rows = jnp.repeat(cut_len, TREE_BLOCK_SIZE)
        own_block = query_block == key_id
        visible = (key_inside[None, :] < cut_rows[:, None]) & (
            jnp.logical_not(own_block)[:, None] | (key_inside[None, :] <= query_inside[:, None])
        )

        def compute(state):
            running, total, weighted = state
            scores = (
                jnp.einsum(
                    "tkgd,skd->kgts",
                    query_grid,
                    key_block.reshape(TREE_BLOCK_SIZE, kv_heads, HEAD_SIZE),
                    preferred_element_type=jnp.float32,
                )
                * scale
            )
            scores = jnp.where(visible[None, None], scores, masked_low)
            new_max = jnp.maximum(running, jnp.max(scores, axis=-1))
            exp_terms = jnp.where(visible[None, None], jnp.exp(scores - new_max[..., None]), 0.0)
            rescale = jnp.exp(running - new_max)
            total = total * rescale + jnp.sum(exp_terms, axis=-1)
            weights = exp_terms.astype(jnp.bfloat16)
            update = jnp.einsum(
                "kgts,skd->tkgd",
                weights,
                val_block.reshape(TREE_BLOCK_SIZE, kv_heads, HEAD_SIZE),
                preferred_element_type=jnp.float32,
            )
            weighted = weighted * jnp.transpose(rescale, (2, 0, 1))[..., None] + update
            return (new_max, total, weighted)

        return lax.cond(jnp.any(visible), compute, lambda unchanged: unchanged, carried)

    initial = (
        jnp.full((kv_heads, head_group_width, row_count), masked_low, jnp.float32),
        jnp.zeros((kv_heads, head_group_width, row_count), jnp.float32),
        jnp.zeros((row_count, kv_heads, head_group_width, HEAD_SIZE), jnp.float32),
    )
    key_rows = lax.all_gather(rotary_keys, ("outer", "inner"), axis=0, tiled=True)
    val_rows = lax.all_gather(values, ("outer", "inner"), axis=0, tiled=True)

    def block_step(slot, state):
        key_block = lax.dynamic_slice_in_dim(key_rows, slot * TREE_BLOCK_SIZE, TREE_BLOCK_SIZE, 0)
        val_block = lax.dynamic_slice_in_dim(val_rows, slot * TREE_BLOCK_SIZE, TREE_BLOCK_SIZE, 0)
        return key_block_step(state, key_block, val_block, slot)

    running, total, weighted = lax.fori_loop(
        0, key_rows.shape[0] // TREE_BLOCK_SIZE, block_step, initial
    )
    attended = weighted / jnp.transpose(total, (2, 0, 1))[..., None]
    attended = attended.reshape(row_count, query_heads * HEAD_SIZE).astype(jnp.bfloat16)
    return lax.all_to_all(attended, "tensor", split_axis=0, concat_axis=1, tiled=True)


MESH = pl.DeviceIdType.MESH


class Halves:
    def __init__(self, half):
        self.parts = [half(0), half(1)]

    def start(self):
        for part in self.parts:
            part.start()

    def wait_send(self):
        for part in self.parts:
            part.wait_send()

    def wait_recv(self):
        for part in self.parts:
            part.wait_recv()


def fused_kernel(
    outer_count, inner_count, tensor_count, listed,
    anc_hbm, cut_hbm, pos_hbm, q_hbm, k_hbm, v_hbm, out_ref,
    anc_ref, cut_ref, pos_ref, q_ref, k_ref,
    kv, turned, own_scores, staged, local_sem, kv_send, kv_pass, kv_recv, out_send, out_recv,
):
    block_count = outer_count * inner_count
    width = q_ref.shape[1]
    heads = width // HEAD_SIZE
    chunk = TREE_BLOCK_SIZE // tensor_count
    rows = heads * chunk
    tensor_me = lax.axis_index("tensor")
    outer_me = lax.axis_index("outer")
    inner_me = lax.axis_index("inner")
    me = outer_me * inner_count + inner_me
    chips = tensor_count // 2

    def tensor_peer(step):
        chip = lax.rem(tensor_me // 2 + step // 2, chips)
        return chip * 2 + lax.rem(lax.rem(tensor_me, 2) + step % 2, 2)

    def tensor_source(step):
        chip = lax.rem(tensor_me // 2 + chips - step // 2, chips)
        return chip * 2 + lax.rem(lax.rem(tensor_me, 2) + step % 2, 2)

    def load(i, source, target):
        return pltpu.make_async_copy(source, target, local_sem.at[i])

    loads = [
        load(0, pos_hbm, pos_ref),
        load(1, k_hbm, k_ref),
        load(2, v_hbm, kv.at[me, pl.ds(TREE_BLOCK_SIZE, TREE_BLOCK_SIZE)]),
        load(3, q_hbm, q_ref),
        load(4, anc_hbm, anc_ref),
        load(5, cut_hbm, cut_ref),
    ]
    for item in loads:
        item.start()

    def reaches(source_inner, target_inner):
        relayed = (lax.rem(source_inner, 2) == 1) & (target_inner - source_inner == 2)
        return (source_inner < target_inner) & jnp.logical_not(relayed)

    barrier = pltpu.get_barrier_semaphore()
    for step in range(1, tensor_count):
        pl.semaphore_signal(barrier, inc=1, device_id={"tensor": tensor_peer(step)}, device_id_type=MESH)
    for z in range(inner_count):
        @pl.when(reaches(z, inner_me))
        def _():
            pl.semaphore_signal(barrier, inc=1, device_id={"inner": z}, device_id_type=MESH)
    for z in range(inner_count):
        @pl.when((outer_me == 1) & (z >= inner_me))
        def _():
            pl.semaphore_signal(barrier, inc=1, device_id={"outer": 0, "inner": z}, device_id_type=MESH)

    lane = lax.broadcasted_iota(jnp.int32, (TREE_BLOCK_SIZE, HEAD_SIZE), 1)
    row = lax.broadcasted_iota(jnp.int32, (TREE_BLOCK_SIZE, HEAD_SIZE), 0)
    half = HEAD_SIZE // 2
    pair = jnp.where(lane < half, lane, lane - half).astype(jnp.float32)
    frequency = jnp.exp(pair[:8] * ((-2.0 / HEAD_SIZE) * math.log(rope_base)))
    near = row[:8].astype(jnp.float32) * frequency
    near_cos, near_sin = jnp.cos(near), jnp.sin(near)
    tiles = TREE_BLOCK_SIZE // 8
    loads[0].wait()
    far_rows = (pos_ref[0] + 8 * row[:tiles]).astype(jnp.float32)
    far = far_rows * frequency[:1]
    far_cos, far_sin = jnp.cos(far), jnp.sin(far)
    cos_parts, sin_parts = [], []
    for tile in range(tiles):
        fc, fs = far_cos[tile : tile + 1], far_sin[tile : tile + 1]
        cos_parts.append(fc * near_cos - fs * near_sin)
        sin_parts.append(fs * near_cos + fc * near_sin)
    cosines = jnp.concatenate(cos_parts, axis=0)
    sines = jnp.concatenate(sin_parts, axis=0)
    sines = jnp.where(lane < half, -sines, sines)

    def rotate(x):
        x = x.astype(jnp.float32)
        return (x * cosines + pltpu.roll(x, half, 1) * sines).astype(jnp.bfloat16)

    loads[1].wait()
    own_keys = rotate(k_ref[...])
    kv[me, :TREE_BLOCK_SIZE] = own_keys
    loads[2].wait()

    sends = inner_count - 1 - inner_me + jnp.where(outer_me == 0, inner_me + 1, 0)
    inner_odd = lax.rem(inner_me, 2) == 1
    relays = jnp.logical_not(inner_odd) & (inner_me >= 2) & (inner_me + 1 < inner_count)
    skips = jnp.where(inner_odd & (inner_me + 2 < inner_count), 1, 0)
    pl.semaphore_wait(barrier, tensor_count - 1 + sends - skips)

    def kv_copy(block, z):
        def half(h):
            part = kv.at[block, pl.ds(h * TREE_BLOCK_SIZE, TREE_BLOCK_SIZE)]
            return pltpu.make_async_remote_copy(
                src_ref=part, dst_ref=part,
                send_sem=kv_send.at[h, z], recv_sem=kv_recv.at[h, block],
                device_id={"inner": z}, device_id_type=MESH,
            )
        return Halves(half)

    def kv_down(z):
        def half(h):
            part = kv.at[me, pl.ds(h * TREE_BLOCK_SIZE, TREE_BLOCK_SIZE)]
            return pltpu.make_async_remote_copy(
                src_ref=part, dst_ref=part,
                send_sem=kv_send.at[h, z], recv_sem=kv_recv.at[h, me],
                device_id={"outer": 1, "inner": z}, device_id_type=MESH,
            )
        return Halves(half)

    def kv_forward(block):
        def half(h):
            part = kv.at[block, pl.ds(h * TREE_BLOCK_SIZE, TREE_BLOCK_SIZE)]
            return pltpu.make_async_remote_copy(
                src_ref=part, dst_ref=part,
                send_sem=kv_pass.at[h, block], recv_sem=kv_recv.at[h, block],
                device_id={"outer": 1}, device_id_type=MESH,
            )
        return Halves(half)

    def kv_relay():
        def half(h):
            part = kv.at[me - 1, pl.ds(h * TREE_BLOCK_SIZE, TREE_BLOCK_SIZE)]
            return pltpu.make_async_remote_copy(
                src_ref=part, dst_ref=part,
                send_sem=kv_pass.at[h, inner_me + 1], recv_sem=kv_recv.at[h, me - 1],
                device_id={"inner": inner_me + 1}, device_id_type=MESH,
            )
        return Halves(half)

    @pl.when(outer_me == 0)
    def _():
        kv_forward(inner_me).start()
    for distance in range(1, inner_count):
        @pl.when((inner_me + distance < inner_count) & reaches(inner_me, inner_me + distance))
        def _():
            kv_copy(me, inner_me + distance).start()
        @pl.when((outer_me == 0) & (inner_me - distance >= 0))
        def _():
            kv_down(inner_me - distance).start()

    def pass_on(distance):
        z = inner_me - distance
        @pl.when((outer_me == 0) & (z >= 0))
        def _():
            for h in range(2):
                kv_copy(z, z).parts[h].wait_recv()
                if distance == 1:
                    @pl.when(relays)
                    def _():
                        kv_relay().parts[h].start()
                kv_forward(z).parts[h].start()
        if distance == 1:
            @pl.when((outer_me == 1) & relays)
            def _():
                for h in range(2):
                    kv_relay().parts[h].wait_recv()
                    kv_relay().parts[h].start()

    loads[3].wait()
    for head in range(heads):
        spun = rotate(q_ref[:, head * HEAD_SIZE : (head + 1) * HEAD_SIZE])
        for c in range(tensor_count):
            turned[c, head * chunk : (head + 1) * chunk] = spun[c * chunk : (c + 1) * chunk]
    for distance in range(1, inner_count):
        pass_on(distance)
    row_in = lax.broadcasted_iota(jnp.int32, (rows, TREE_BLOCK_SIZE), 0) % chunk
    key_in = lax.broadcasted_iota(jnp.int32, (rows, TREE_BLOCK_SIZE), 1)
    contract_last = (((1,), (1,)), ((), ()))
    for c in range(tensor_count):
        s = lax.dot_general(turned[c], own_keys, contract_last, preferred_element_type=jnp.float32)
        own_scores[c] = jnp.where(key_in <= row_in + c * chunk, s, masked_low)

    for j in range(block_count - 1):
        @pl.when((outer_me == 1) & (j < me) & jnp.logical_not(relays & (j == me - 1)))
        def _():
            kv_copy(j, inner_me).wait_recv()
    loads[4].wait()
    loads[5].wait()

    key_parts, val_parts, seen = [], [kv[me][TREE_BLOCK_SIZE:]], []
    for e in range(1, listed):
        index = jnp.maximum(anc_ref[0, e], 0)
        pair_block = kv[index]
        key_parts.append(pair_block[:TREE_BLOCK_SIZE])
        val_parts.append(pair_block[TREE_BLOCK_SIZE:])
        seen.append(key_in < cut_ref[0, e])
    far_keys = jnp.concatenate(key_parts, axis=0)
    all_vals = jnp.concatenate(val_parts, axis=0)
    factor = math.log2(math.e) / math.sqrt(HEAD_SIZE)

    def out_copy(step, column):
        return pltpu.make_async_remote_copy(
            src_ref=staged.at[step],
            dst_ref=out_ref.at[:, pl.ds(pl.multiple_of(column * width, width), width)],
            send_sem=out_send.at[step], recv_sem=out_recv.at[step],
            device_id={"tensor": tensor_peer(step)}, device_id_type=MESH,
        )

    for step in send_order(tensor_count):
        c = tensor_peer(step)
        s = lax.dot_general(turned[c], far_keys, contract_last, preferred_element_type=jnp.float32)
        parts = [own_scores[c]]
        for e in range(listed - 1):
            part = s[:, e * TREE_BLOCK_SIZE : (e + 1) * TREE_BLOCK_SIZE]
            parts.append(jnp.where(seen[e], part, masked_low))
        top = functools.reduce(jnp.maximum, parts)
        row_max = jnp.max(top, axis=1, keepdims=True)
        terms = [jnp.exp2((part - row_max) * factor) for part in parts]
        total = jnp.sum(functools.reduce(jnp.add, terms), axis=1, keepdims=True)
        weights = jnp.concatenate([t.astype(jnp.bfloat16) for t in terms], axis=1)
        summed = jnp.dot(weights, all_vals, preferred_element_type=jnp.float32)
        result = (summed / total).astype(jnp.bfloat16)
        for head in range(heads):
            piece = result[head * chunk : (head + 1) * chunk]
            if step == 0:
                column = tensor_me * width + head * HEAD_SIZE
                out_ref[:, pl.ds(pl.multiple_of(column, HEAD_SIZE), HEAD_SIZE)] = piece
            else:
                staged[step, :, head * HEAD_SIZE : (head + 1) * HEAD_SIZE] = piece
        if step != 0:
            out_copy(step, tensor_me).start()

    for z in range(inner_count):
        @pl.when(reaches(inner_me, z))
        def _():
            kv_copy(me, z).wait_send()
        @pl.when((outer_me == 0) & (z < inner_me))
        def _():
            kv_down(z).wait_send()
        @pl.when((outer_me == 0) & (z <= inner_me))
        def _():
            kv_forward(z).wait_send()
    @pl.when(relays)
    def _():
        kv_relay().wait_send()
    for step in range(1, tensor_count):
        copy = out_copy(step, tensor_source(step))
        copy.wait_send()
        copy.wait_recv()


def send_order(tensor_count):
    return list(range(tensor_count - 1, -1, -1))


def fused(sizes, queries, keys, values, ancestors, visible_cut, positions):
    outer_count, inner_count, tensor_count = sizes
    block_count = outer_count * inner_count
    width = queries.shape[1]
    heads = width // HEAD_SIZE
    chunk = TREE_BLOCK_SIZE // tensor_count
    listed = ancestors.shape[1]
    hbm = pl.BlockSpec(memory_space=pltpu.HBM)
    return pl.pallas_call(
        functools.partial(fused_kernel, outer_count, inner_count, tensor_count, listed),
        out_shape=jax.ShapeDtypeStruct((chunk, width * tensor_count), jnp.bfloat16),
        in_specs=[hbm] * 6,
        out_specs=pl.BlockSpec(memory_space=pltpu.VMEM),
        scratch_shapes=[
            pltpu.SMEM(ancestors.shape, jnp.int32),
            pltpu.SMEM(visible_cut.shape, jnp.int32),
            pltpu.SMEM(positions.shape, jnp.int32),
            pltpu.VMEM(queries.shape, jnp.bfloat16),
            pltpu.VMEM(keys.shape, jnp.bfloat16),
            pltpu.VMEM((block_count, 2 * TREE_BLOCK_SIZE, HEAD_SIZE), jnp.bfloat16),
            pltpu.VMEM((tensor_count, heads * chunk, HEAD_SIZE), jnp.bfloat16),
            pltpu.VMEM((tensor_count, heads * chunk, TREE_BLOCK_SIZE), jnp.float32),
            pltpu.VMEM((tensor_count, chunk, width), jnp.bfloat16),
            pltpu.SemaphoreType.DMA((6,)),
            pltpu.SemaphoreType.DMA((2, inner_count)),
            pltpu.SemaphoreType.DMA((2, inner_count)),
            pltpu.SemaphoreType.DMA((2, block_count)),
            pltpu.SemaphoreType.DMA((tensor_count,)),
            pltpu.SemaphoreType.DMA((tensor_count,)),
        ],
        compiler_params=pltpu.CompilerParams(
            collective_id=0, has_side_effects=True, vmem_limit_bytes=64 * 1024 * 1024
        ),
    )(ancestors, visible_cut, positions, queries, keys, values)


def pick(sizes, queries, keys, *rest):
    small = (
        queries.shape[0] == TREE_BLOCK_SIZE
        and keys.shape[1] == HEAD_SIZE
        and sizes[0] == 2
        and sizes[1] <= 8
        and sizes[2] % 2 == 0
        and rest[1].shape[1] <= 8
    )
    body = functools.partial(fused, sizes) if small else local
    return body(queries, keys, *rest)


def solution(mesh):
    placed = (
        P(("outer", "inner"), "tensor"),
        P(("outer", "inner"), "tensor"),
        P(("outer", "inner"), "tensor"),
        P(("outer", "inner"), None),
        P(("outer", "inner"), None),
        P(("outer", "inner")),
    )
    sizes = tuple(mesh.shape[name] for name in ("outer", "inner", "tensor"))
    return jax.shard_map(
        functools.partial(pick, sizes),
        mesh=mesh,
        in_specs=placed,
        out_specs=P(("outer", "inner", "tensor"), None),
        check_vma=False,
    )
```

```python
import functools
import math

import jax
import jax.numpy as jnp
from jax import lax
from jax.experimental import pallas as pl
from jax.experimental.pallas import tpu as pltpu
from jax.sharding import PartitionSpec as P

HEAD_SIZE = 128
TREE_BLOCK_SIZE = 128


rope_base = 500000.0
masked_low = -1e30


def apply_rotary(source, positions, head_count):
    token_count = source.shape[0]
    half_dim = HEAD_SIZE // 2
    frequency = jnp.exp(
        jnp.arange(half_dim, dtype=jnp.float32) * (-2.0 / HEAD_SIZE) * math.log(rope_base)
    )
    angles = positions.astype(jnp.float32)[:, None] * frequency[None, :]
    cosines = jnp.cos(angles)[:, None, :]
    sine_vals = jnp.sin(angles)[:, None, :]
    split_heads = source.astype(jnp.float32).reshape(token_count, head_count, HEAD_SIZE)
    front_half = split_heads[..., :half_dim]
    back_half = split_heads[..., half_dim:]
    turned = jnp.concatenate(
        [
            front_half * cosines - back_half * sine_vals,
            back_half * cosines + front_half * sine_vals,
        ],
        axis=-1,
    )
    return turned.reshape(token_count, head_count * HEAD_SIZE).astype(jnp.bfloat16)


def local(queries, keys, values, ancestors, visible_cut, positions):
    row_count = queries.shape[0]
    query_heads = queries.shape[1] // HEAD_SIZE
    kv_heads = keys.shape[1] // HEAD_SIZE
    head_group_width = query_heads // kv_heads
    scale = 1.0 / math.sqrt(HEAD_SIZE)
    rotary_queries = apply_rotary(queries, positions, query_heads)
    rotary_keys = apply_rotary(keys, positions, kv_heads)
    query_grid = rotary_queries.reshape(row_count, kv_heads, head_group_width, HEAD_SIZE)
    first_block = lax.axis_index(("outer", "inner")) * (row_count // TREE_BLOCK_SIZE)
    query_block = first_block + jnp.arange(row_count, dtype=jnp.int32) // TREE_BLOCK_SIZE
    query_inside = jnp.arange(row_count, dtype=jnp.int32) % TREE_BLOCK_SIZE
    key_inside = jnp.arange(TREE_BLOCK_SIZE, dtype=jnp.int32)

    def key_block_step(carried, key_block, val_block, key_id):
        cut_len = jnp.sum(jnp.where(ancestors == key_id, visible_cut, 0), axis=1)
        cut_rows = jnp.repeat(cut_len, TREE_BLOCK_SIZE)
        own_block = query_block == key_id
        visible = (key_inside[None, :] < cut_rows[:, None]) & (
            jnp.logical_not(own_block)[:, None] | (key_inside[None, :] <= query_inside[:, None])
        )

        def compute(state):
            running, total, weighted = state
            scores = (
                jnp.einsum(
                    "tkgd,skd->kgts",
                    query_grid,
                    key_block.reshape(TREE_BLOCK_SIZE, kv_heads, HEAD_SIZE),
                    preferred_element_type=jnp.float32,
                )
                * scale
            )
            scores = jnp.where(visible[None, None], scores, masked_low)
            new_max = jnp.maximum(running, jnp.max(scores, axis=-1))
            exp_terms = jnp.where(visible[None, None], jnp.exp(scores - new_max[..., None]), 0.0)
            rescale = jnp.exp(running - new_max)
            total = total * rescale + jnp.sum(exp_terms, axis=-1)
            weights = exp_terms.astype(jnp.bfloat16)
            update = jnp.einsum(
                "kgts,skd->tkgd",
                weights,
                val_block.reshape(TREE_BLOCK_SIZE, kv_heads, HEAD_SIZE),
                preferred_element_type=jnp.float32,
            )
            weighted = weighted * jnp.transpose(rescale, (2, 0, 1))[..., None] + update
            return (new_max, total, weighted)

        return lax.cond(jnp.any(visible), compute, lambda unchanged: unchanged, carried)

    initial = (
        jnp.full((kv_heads, head_group_width, row_count), masked_low, jnp.float32),
        jnp.zeros((kv_heads, head_group_width, row_count), jnp.float32),
        jnp.zeros((row_count, kv_heads, head_group_width, HEAD_SIZE), jnp.float32),
    )
    key_rows = lax.all_gather(rotary_keys, ("outer", "inner"), axis=0, tiled=True)
    val_rows = lax.all_gather(values, ("outer", "inner"), axis=0, tiled=True)

    def block_step(slot, state):
        key_block = lax.dynamic_slice_in_dim(key_rows, slot * TREE_BLOCK_SIZE, TREE_BLOCK_SIZE, 0)
        val_block = lax.dynamic_slice_in_dim(val_rows, slot * TREE_BLOCK_SIZE, TREE_BLOCK_SIZE, 0)
        return key_block_step(state, key_block, val_block, slot)

    running, total, weighted = lax.fori_loop(
        0, key_rows.shape[0] // TREE_BLOCK_SIZE, block_step, initial
    )
    attended = weighted / jnp.transpose(total, (2, 0, 1))[..., None]
    attended = attended.reshape(row_count, query_heads * HEAD_SIZE).astype(jnp.bfloat16)
    return lax.all_to_all(attended, "tensor", split_axis=0, concat_axis=1, tiled=True)


MESH = pl.DeviceIdType.MESH


class Halves:
    def __init__(self, half):
        self.parts = [half(0), half(1)]

    def start(self):
        for part in self.parts:
            part.start()

    def wait_send(self):
        for part in self.parts:
            part.wait_send()

    def wait_recv(self):
        for part in self.parts:
            part.wait_recv()


def fused_kernel(
    outer_count, inner_count, tensor_count, listed,
    anc_hbm, cut_hbm, pos_hbm, q_hbm, k_hbm, v_hbm, out_ref,
    anc_ref, cut_ref, pos_ref, q_ref, k_ref,
    kv, turned, own_scores, staged, local_sem, kv_send, kv_pass, kv_recv, out_send, out_recv,
):
    block_count = outer_count * inner_count
    width = q_ref.shape[1]
    heads = width // HEAD_SIZE
    chunk = TREE_BLOCK_SIZE // tensor_count
    rows = heads * chunk
    tensor_me = lax.axis_index("tensor")
    outer_me = lax.axis_index("outer")
    inner_me = lax.axis_index("inner")
    me = outer_me * inner_count + inner_me
    chips = tensor_count // 2

    def tensor_peer(step):
        chip = lax.rem(tensor_me // 2 + step // 2, chips)
        return chip * 2 + lax.rem(lax.rem(tensor_me, 2) + step % 2, 2)

    def tensor_source(step):
        chip = lax.rem(tensor_me // 2 + chips - step // 2, chips)
        return chip * 2 + lax.rem(lax.rem(tensor_me, 2) + step % 2, 2)

    def load(i, source, target):
        return pltpu.make_async_copy(source, target, local_sem.at[i])

    loads = [
        load(0, pos_hbm, pos_ref),
        load(1, k_hbm, k_ref),
        load(2, v_hbm, kv.at[me, pl.ds(TREE_BLOCK_SIZE, TREE_BLOCK_SIZE)]),
        load(3, q_hbm, q_ref),
        load(4, anc_hbm, anc_ref),
        load(5, cut_hbm, cut_ref),
    ]
    for item in loads:
        item.start()

    def reaches(source_inner, target_inner):
        relayed = (lax.rem(source_inner, 2) == 1) & (target_inner - source_inner == 2)
        return (source_inner < target_inner) & jnp.logical_not(relayed)

    barrier = pltpu.get_barrier_semaphore()
    for step in range(1, tensor_count):
        pl.semaphore_signal(barrier, inc=1, device_id={"tensor": tensor_peer(step)}, device_id_type=MESH)
    for z in range(inner_count):
        @pl.when(reaches(z, inner_me))
        def _():
            pl.semaphore_signal(barrier, inc=1, device_id={"inner": z}, device_id_type=MESH)
    for z in range(inner_count):
        @pl.when((outer_me == 1) & (z >= inner_me))
        def _():
            pl.semaphore_signal(barrier, inc=1, device_id={"outer": 0, "inner": z}, device_id_type=MESH)

    lane = lax.broadcasted_iota(jnp.int32, (TREE_BLOCK_SIZE, HEAD_SIZE), 1)
    row = lax.broadcasted_iota(jnp.int32, (TREE_BLOCK_SIZE, HEAD_SIZE), 0)
    half = HEAD_SIZE // 2
    pair = jnp.where(lane < half, lane, lane - half).astype(jnp.float32)
    frequency = jnp.exp(pair[:8] * ((-2.0 / HEAD_SIZE) * math.log(rope_base)))
    near = row[:8].astype(jnp.float32) * frequency
    near_cos, near_sin = jnp.cos(near), jnp.sin(near)
    tiles = TREE_BLOCK_SIZE // 8
    loads[0].wait()
    far_rows = (pos_ref[0] + 8 * row[:tiles]).astype(jnp.float32)
    far = far_rows * frequency[:1]
    far_cos, far_sin = jnp.cos(far), jnp.sin(far)
    cos_parts, sin_parts = [], []
    for tile in range(tiles):
        fc, fs = far_cos[tile : tile + 1], far_sin[tile : tile + 1]
        cos_parts.append(fc * near_cos - fs * near_sin)
        sin_parts.append(fs * near_cos + fc * near_sin)
    cosines = jnp.concatenate(cos_parts, axis=0)
    sines = jnp.concatenate(sin_parts, axis=0)
    sines = jnp.where(lane < half, -sines, sines)

    def rotate(x):
        x = x.astype(jnp.float32)
        return (x * cosines + pltpu.roll(x, half, 1) * sines).astype(jnp.bfloat16)

    loads[1].wait()
    own_keys = rotate(k_ref[...])
    kv[me, :TREE_BLOCK_SIZE] = own_keys
    loads[2].wait()

    sends = inner_count - 1 - inner_me + jnp.where(outer_me == 0, inner_me + 1, 0)
    inner_odd = lax.rem(inner_me, 2) == 1
    relays = jnp.logical_not(inner_odd) & (inner_me >= 2) & (inner_me + 1 < inner_count)
    skips = jnp.where(inner_odd & (inner_me + 2 < inner_count), 1, 0)
    pl.semaphore_wait(barrier, tensor_count - 1 + sends - skips)

    def kv_copy(block, z):
        def half(h):
            part = kv.at[block, pl.ds(h * TREE_BLOCK_SIZE, TREE_BLOCK_SIZE)]
            return pltpu.make_async_remote_copy(
                src_ref=part, dst_ref=part,
                send_sem=kv_send.at[h, z], recv_sem=kv_recv.at[h, block],
                device_id={"inner": z}, device_id_type=MESH,
            )
        return Halves(half)

    def kv_down(z):
        def half(h):
            part = kv.at[me, pl.ds(h * TREE_BLOCK_SIZE, TREE_BLOCK_SIZE)]
            return pltpu.make_async_remote_copy(
                src_ref=part, dst_ref=part,
                send_sem=kv_send.at[h, z], recv_sem=kv_recv.at[h, me],
                device_id={"outer": 1, "inner": z}, device_id_type=MESH,
            )
        return Halves(half)

    def kv_forward(block):
        def half(h):
            part = kv.at[block, pl.ds(h * TREE_BLOCK_SIZE, TREE_BLOCK_SIZE)]
            return pltpu.make_async_remote_copy(
                src_ref=part, dst_ref=part,
                send_sem=kv_pass.at[h, block], recv_sem=kv_recv.at[h, block],
                device_id={"outer": 1}, device_id_type=MESH,
            )
        return Halves(half)

    def kv_relay():
        def half(h):
            part = kv.at[me - 1, pl.ds(h * TREE_BLOCK_SIZE, TREE_BLOCK_SIZE)]
            return pltpu.make_async_remote_copy(
                src_ref=part, dst_ref=part,
                send_sem=kv_pass.at[h, inner_me + 1], recv_sem=kv_recv.at[h, me - 1],
                device_id={"inner": inner_me + 1}, device_id_type=MESH,
            )
        return Halves(half)

    @pl.when(outer_me == 0)
    def _():
        kv_forward(inner_me).start()
    for distance in range(1, inner_count):
        @pl.when((inner_me + distance < inner_count) & reaches(inner_me, inner_me + distance))
        def _():
            kv_copy(me, inner_me + distance).start()
        @pl.when((outer_me == 0) & (inner_me - distance >= 0))
        def _():
            kv_down(inner_me - distance).start()

    def pass_on(distance):
        z = inner_me - distance
        @pl.when((outer_me == 0) & (z >= 0))
        def _():
            for h in range(2):
                kv_copy(z, z).parts[h].wait_recv()
                if distance == 1:
                    @pl.when(relays)
                    def _():
                        kv_relay().parts[h].start()
                kv_forward(z).parts[h].start()
        if distance == 1:
            @pl.when((outer_me == 1) & relays)
            def _():
                for h in range(2):
                    kv_relay().parts[h].wait_recv()
                    kv_relay().parts[h].start()

    pass_on(1)
    loads[3].wait()
    for head in range(heads):
        spun = rotate(q_ref[:, head * HEAD_SIZE : (head + 1) * HEAD_SIZE])
        for c in range(tensor_count):
            turned[c, head * chunk : (head + 1) * chunk] = spun[c * chunk : (c + 1) * chunk]
    for distance in range(2, inner_count):
        pass_on(distance)
    row_in = lax.broadcasted_iota(jnp.int32, (rows, TREE_BLOCK_SIZE), 0) % chunk
    key_in = lax.broadcasted_iota(jnp.int32, (rows, TREE_BLOCK_SIZE), 1)
    contract_last = (((1,), (1,)), ((), ()))
    for c in range(tensor_count):
        s = lax.dot_general(turned[c], own_keys, contract_last, preferred_element_type=jnp.float32)
        own_scores[c] = jnp.where(key_in <= row_in + c * chunk, s, masked_low)

    for j in range(block_count - 1):
        @pl.when((outer_me == 1) & (j < me) & jnp.logical_not(relays & (j == me - 1)))
        def _():
            kv_copy(j, inner_me).wait_recv()
    loads[4].wait()
    loads[5].wait()

    key_parts, val_parts, seen = [], [kv[me][TREE_BLOCK_SIZE:]], []
    for e in range(1, listed):
        index = jnp.maximum(anc_ref[0, e], 0)
        pair_block = kv[index]
        key_parts.append(pair_block[:TREE_BLOCK_SIZE])
        val_parts.append(pair_block[TREE_BLOCK_SIZE:])
        seen.append(key_in < cut_ref[0, e])
    far_keys = jnp.concatenate(key_parts, axis=0)
    all_vals = jnp.concatenate(val_parts, axis=0)
    factor = math.log2(math.e) / math.sqrt(HEAD_SIZE)

    def out_copy(step, column):
        return pltpu.make_async_remote_copy(
            src_ref=staged.at[step],
            dst_ref=out_ref.at[:, pl.ds(pl.multiple_of(column * width, width), width)],
            send_sem=out_send.at[step], recv_sem=out_recv.at[step],
            device_id={"tensor": tensor_peer(step)}, device_id_type=MESH,
        )

    for step in send_order(tensor_count):
        c = tensor_peer(step)
        s = lax.dot_general(turned[c], far_keys, contract_last, preferred_element_type=jnp.float32)
        parts = [own_scores[c]]
        for e in range(listed - 1):
            part = s[:, e * TREE_BLOCK_SIZE : (e + 1) * TREE_BLOCK_SIZE]
            parts.append(jnp.where(seen[e], part, masked_low))
        top = functools.reduce(jnp.maximum, parts)
        row_max = jnp.max(top, axis=1, keepdims=True)
        terms = [jnp.exp2((part - row_max) * factor) for part in parts]
        total = jnp.sum(functools.reduce(jnp.add, terms), axis=1, keepdims=True)
        weights = jnp.concatenate([t.astype(jnp.bfloat16) for t in terms], axis=1)
        summed = jnp.dot(weights, all_vals, preferred_element_type=jnp.float32)
        result = (summed / total).astype(jnp.bfloat16)
        for head in range(heads):
            piece = result[head * chunk : (head + 1) * chunk]
            if step == 0:
                column = tensor_me * width + head * HEAD_SIZE
                out_ref[:, pl.ds(pl.multiple_of(column, HEAD_SIZE), HEAD_SIZE)] = piece
            else:
                staged[step, :, head * HEAD_SIZE : (head + 1) * HEAD_SIZE] = piece
        if step != 0:
            out_copy(step, tensor_me).start()

    for z in range(inner_count):
        @pl.when(reaches(inner_me, z))
        def _():
            kv_copy(me, z).wait_send()
        @pl.when((outer_me == 0) & (z < inner_me))
        def _():
            kv_down(z).wait_send()
        @pl.when((outer_me == 0) & (z <= inner_me))
        def _():
            kv_forward(z).wait_send()
    @pl.when(relays)
    def _():
        kv_relay().wait_send()
    for step in range(1, tensor_count):
        copy = out_copy(step, tensor_source(step))
        copy.wait_send()
        copy.wait_recv()


def send_order(tensor_count):
    return list(range(tensor_count - 1, -1, -1))


def fused(sizes, queries, keys, values, ancestors, visible_cut, positions):
    outer_count, inner_count, tensor_count = sizes
    block_count = outer_count * inner_count
    width = queries.shape[1]
    heads = width // HEAD_SIZE
    chunk = TREE_BLOCK_SIZE // tensor_count
    listed = ancestors.shape[1]
    hbm = pl.BlockSpec(memory_space=pltpu.HBM)
    return pl.pallas_call(
        functools.partial(fused_kernel, outer_count, inner_count, tensor_count, listed),
        out_shape=jax.ShapeDtypeStruct((chunk, width * tensor_count), jnp.bfloat16),
        in_specs=[hbm] * 6,
        out_specs=pl.BlockSpec(memory_space=pltpu.VMEM),
        scratch_shapes=[
            pltpu.SMEM(ancestors.shape, jnp.int32),
            pltpu.SMEM(visible_cut.shape, jnp.int32),
            pltpu.SMEM(positions.shape, jnp.int32),
            pltpu.VMEM(queries.shape, jnp.bfloat16),
            pltpu.VMEM(keys.shape, jnp.bfloat16),
            pltpu.VMEM((block_count, 2 * TREE_BLOCK_SIZE, HEAD_SIZE), jnp.bfloat16),
            pltpu.VMEM((tensor_count, heads * chunk, HEAD_SIZE), jnp.bfloat16),
            pltpu.VMEM((tensor_count, heads * chunk, TREE_BLOCK_SIZE), jnp.float32),
            pltpu.VMEM((tensor_count, chunk, width), jnp.bfloat16),
            pltpu.SemaphoreType.DMA((6,)),
            pltpu.SemaphoreType.DMA((2, inner_count)),
            pltpu.SemaphoreType.DMA((2, inner_count)),
            pltpu.SemaphoreType.DMA((2, block_count)),
            pltpu.SemaphoreType.DMA((tensor_count,)),
            pltpu.SemaphoreType.DMA((tensor_count,)),
        ],
        compiler_params=pltpu.CompilerParams(
            collective_id=0, has_side_effects=True, vmem_limit_bytes=64 * 1024 * 1024
        ),
    )(ancestors, visible_cut, positions, queries, keys, values)


def pick(sizes, queries, keys, *rest):
    small = (
        queries.shape[0] == TREE_BLOCK_SIZE
        and keys.shape[1] == HEAD_SIZE
        and sizes[0] == 2
        and sizes[1] <= 8
        and sizes[2] % 2 == 0
        and rest[1].shape[1] <= 8
    )
    body = functools.partial(fused, sizes) if small else local
    return body(queries, keys, *rest)


def solution(mesh):
    placed = (
        P(("outer", "inner"), "tensor"),
        P(("outer", "inner"), "tensor"),
        P(("outer", "inner"), "tensor"),
        P(("outer", "inner"), None),
        P(("outer", "inner"), None),
        P(("outer", "inner")),
    )
    sizes = tuple(mesh.shape[name] for name in ("outer", "inner", "tensor"))
    return jax.shard_map(
        functools.partial(pick, sizes),
        mesh=mesh,
        in_specs=placed,
        out_specs=P(("outer", "inner", "tensor"), None),
        check_vma=False,
    )
```
